256 devices in a mesh: lon: 16 (over x_lo, z), lat: 16 (over x_hi, y, core).
Axes of the slice: x: 4 (x_hi: 2, x_lo: 2; x = x_hi * 2 + x_lo), y: 4, z: 8, core: 2. Of those that a mesh axis runs over, the one named last changes fastest.
Arguments:
- tracers: float32 [4, 8, 512, 2048], P(None, None, 'lat', 'lon'), may hold values from -6 to 6
- zonal_flow: float32 [8, 512, 2048], P(None, 'lat', 'lon'), may hold values from -0.4 to 0.4
- meridional: float32 [8, 512, 2048], P(None, 'lat', 'lon'), may hold values from -0.4 to 0.4
- land_mask: int32 [512, 2048], P('lat', 'lon'), may hold values from 0 to 1, as said below
- levels: int32 [512, 2048], P('lat', 'lon'), may hold values from 1 to 8
Outputs:
- advanced: float32 [4, 8, 512, 2048], P(None, None, 'lat', 'lon')
The draws below stay inside these ranges and needn't reach their ends.
Inputs may be any that keep to these rules, and one draw needn't show every extreme that they name: `land_mask`: 1 marks sea; land takes scattered points and some whole blocks of 32 x 128 points aligned with the tiles.
All inputs are finite; a program needn't handle non-finite values.
Results may differ from the reference program's by a relative error of at most 0.0003.
Values sent between devices are 32-bit elements; how exact they have to be, the bound alone decides.
No kernel may reach another device: no remote copies, remote signals or barrier semaphores. Data moves between devices by JAX's collectives and lax.ppermute only.
A program may use at most 64 MiB of HBM per device.

```python
import jax
import jax.numpy as jnp
from jax import lax

CX = 128
CY = 32
K = 8
NTRAC = 4
STEPS = 2
NX = 2048
NY = 512


def draw_land_mask(key, part):
    key = jax.random.fold_in(key, 11)
    block_key, point_key = jax.random.split(key)
    blocks = jax.random.randint(block_key, (NY // CY, NX // CX), 0, 4)
    coarse = jnp.repeat(jnp.repeat(blocks, CY, axis=0), CX, axis=1)
    points = jax.random.randint(point_key, (NY, NX), 0, 8)
    return jnp.where((coarse == 0) | (points == 0), 0, 1).astype(jnp.int32)


def plant(values, stream_key, low, high):
    dims = values.shape
    place = [jax.random.randint(jax.random.fold_in(stream_key, axis), (), 0, dims[axis]) for axis in range(len(dims))]
    values = values.at[tuple(place)].set(low)
    longest = dims.index(max(dims))
    place[longest] = (place[longest] + 1) % dims[longest]
    return values.at[tuple(place)].set(high)


def shard_levels(rng, extent, shards, smallest, top_value):
    level, own = 1.0, jax.random.fold_in(rng, 6)
    for axis_at, blocks in shards:
        steps = jnp.exp(jax.random.uniform(jax.random.fold_in(own, axis_at), (blocks,), jnp.float32, smallest / len(shards), top_value / len(shards)))
        level = level * jnp.repeat(steps, extent[axis_at] // blocks).reshape([-1 if axis == axis_at else 1 for axis in range(len(extent))])
    return level


def noise(own_key, extent, scale, limit, cuts=(), kind=jnp.bfloat16):
    entries = scale * jax.random.normal(own_key, extent, jnp.float32)
    if cuts:
        entries = entries * shard_levels(own_key, extent, cuts, -0.22, 0.18)
    return jnp.clip(entries, -limit, limit).astype(kind)


def setup_inputs(seed: int = 0) -> dict:
    arg_keys = jax.random.split(jax.random.key(seed), 6)
    tracers = noise(arg_keys[0], (NTRAC, K, NY, NX), 1.0, 6.0, ((2, 16), (3, 16)), jnp.float32)
    zonal_flow = jnp.clip(jax.random.uniform(arg_keys[1], (K, NY, NX), jnp.float32, -0.4, 0.4) * shard_levels(arg_keys[1], (K, NY, NX), ((1, 16), (2, 16)), -0.4, 0.0), -0.4, 0.4)
    meridional = jnp.clip(jax.random.uniform(arg_keys[2], (K, NY, NX), jnp.float32, -0.4, 0.4) * shard_levels(arg_keys[2], (K, NY, NX), ((1, 16), (2, 16)), -0.4, 0.0), -0.4, 0.4)
    land_mask = draw_land_mask(jax.random.fold_in(arg_keys[5], 71), 0)
    levels = plant(jax.random.randint(arg_keys[4], (NY, NX), 1, K + 1), jax.random.fold_in(arg_keys[4], 1), 1, K).astype(jnp.int32)
    return dict(tracers=tracers, zonal_flow=zonal_flow, meridional=meridional, land_mask=land_mask, levels=levels)


horizontal_diffusion = 0.1
vertical_diffusion = 0.2
upstream_weight = 1.0 / 6.0


def take_range(values, start, stop, along):
    return lax.slice_in_dim(values, start, stop, axis=values.ndim + along)


def divergence(tracer_ext, wet_ext, flow_ext, along):
    length = tracer_ext.shape[along] - 4
    face_wet = take_range(wet_ext, 0, length + 3, along) * take_range(wet_ext, 1, length + 4, along)
    gradient = (take_range(tracer_ext, 1, length + 4, along) - take_range(tracer_ext, 0, length + 3, along)) * face_wet
    curvature = take_range(gradient, 1, length + 3, along) - take_range(gradient, 0, length + 2, along)
    transport = 0.5 * (take_range(flow_ext, 1, length + 2, along) + take_range(flow_ext, 2, length + 3, along)) * take_range(face_wet, 1, length + 2, along)
    face_value = 0.5 * (take_range(tracer_ext, 1, length + 2, along) + take_range(tracer_ext, 2, length + 3, along)) - upstream_weight * jnp.where(transport > 0, take_range(curvature, 0, length + 1, along), take_range(curvature, 1, length + 2, along))
    face_flux = transport * face_value - horizontal_diffusion * take_range(gradient, 1, length + 2, along)
    return take_range(face_flux, 0, length, along) - take_range(face_flux, 1, length + 1, along)


def vertical_mix(tracer, wetness):
    face_wet = wetness[:-1] * wetness[1:]
    gradient = (tracer[..., 1:, :, :] - tracer[..., :-1, :, :]) * face_wet
    zeros = jnp.zeros_like(gradient[..., :1, :, :])
    return vertical_diffusion * (jnp.concatenate([gradient, zeros], -3) - jnp.concatenate([zeros, gradient], -3))


def advance(tracer, tracer_x, tracer_y, wetness, wet_x, zonal_x, wet_y, merid_y):
    return wetness * (tracer + divergence(tracer_x, wet_x, zonal_x, -1) + divergence(tracer_y, wet_y, merid_y, -2) + vertical_mix(tracer, wetness))


def extend_lon(values):
    return jnp.concatenate([values[..., -2:], values, values[..., :2]], -1)


def extend_lat(values, sign):
    rows = values.shape[-2]
    mirrored = jnp.flip(jnp.flip(values[..., rows - 2:, :], -2), -1) * sign
    zeros = jnp.zeros_like(values[..., :2, :])
    return jnp.concatenate([zeros, values, mirrored], -2)


def reference(tracers, zonal_flow, meridional, land_mask, levels):
    depth_index = lax.broadcasted_iota(jnp.int32, zonal_flow.shape, 0)
    wetness = ((land_mask[None] == 1) & (depth_index < levels[None])).astype(jnp.float32)
    wet_x = extend_lon(wetness)
    zonal_x = extend_lon(zonal_flow)
    wet_y = extend_lat(wetness, 1.0)
    merid_y = extend_lat(meridional, -1.0)

    def one_tracer(tracer):
        for step_index in range(STEPS):
            tracer = advance(tracer, extend_lon(tracer), extend_lat(tracer, 1.0), wetness, wet_x, zonal_x, wet_y, merid_y)
        return tracer

    return lax.map(one_tracer, tracers)
```

```python
import jax
import jax.numpy as jnp
from jax import lax
from jax.experimental import pallas as pl
from jax.experimental.pallas import tpu as pltpu
from jax.sharding import PartitionSpec as P


KZ = 8
ROWS = 32
COLS = 128
NT = 4
HALO = 4
EXT = ROWS + 2 * HALO
PAYLOAD = 33

DIFF_H = 0.1
DIFF_V = 0.2
UPSTREAM = 1.0 / 6.0

VREG = (KZ, COLS)


def lanes():
    return lax.broadcasted_iota(jnp.int32, VREG, 1)


def levels_iota():
    return lax.broadcasted_iota(jnp.int32, VREG, 0)


def roll_x(v, shift):
    shift %= COLS
    return v if shift == 0 else pltpu.roll(v, shift, 1)


def roll_k(v, shift):
    return pltpu.roll(v, shift % KZ, 0)


def load_row(ref, y):
    return ref[pl.ds(y, KZ, stride=ROWS), :]


def load_tracer(ref, t, y):
    return ref[t, pl.ds(y, KZ, stride=ROWS), :]


def load_wet(land_ref, levels_ref, y):
    depth = jnp.where(land_ref[pl.ds(y, 1), :] == 1, levels_ref[pl.ds(y, 1), :], 0)
    return jnp.where(levels_iota() < jnp.broadcast_to(depth, VREG), 1.0, 0.0)


def gather_edges(parts):
    slot = ((lanes() - 16) >> 5) & 3
    out = roll_x(parts[-1], 32 * len(parts))
    for t in range(len(parts) - 1):
        out = jnp.where(slot == t, roll_x(parts[t], 32 * (t + 1)), out)
    return out


def row_edges(refs, y):
    tracers, zonal, merid, land, levels = refs
    moving = gather_edges([load_tracer(tracers, t, y) for t in range(NT)])
    static = gather_edges(
        [load_row(zonal, y), load_row(merid, y), load_wet(land, levels, y)]
    )
    return moving, static


def pack_lon_kernel(tracers, zonal, merid, land, levels, a_ref, b_ref):
    refs = (tracers, zonal, merid, land, levels)
    even = lax.rem(lax.axis_index("lon"), 2) == 0
    lane = lanes()
    to_right = ((lane - 28) >> 2) & 7
    to_left = (lane >> 2) & 7
    for g in range(ROWS // 8):
        right, left = [None, None], [None, None]
        for r in range(8):
            for i, edge in enumerate(row_edges(refs, 8 * g + r)):
                moved = roll_x(edge, 4 * r)
                right[i] = moved if r == 0 else jnp.where(to_right == r, moved, right[i])
                left[i] = moved if r == 0 else jnp.where(to_left == r, moved, left[i])
        for i in range(2):
            a_ref[i, g] = jnp.where(even, right[i], left[i])
            b_ref[i, g] = jnp.where(even, left[i], right[i])


def pack_lat_kernel(
    tracers, zonal, merid, land, levels, ra_ref, rb_ref, a_ref, b_ref, edge_ref
):
    refs = (tracers, zonal, merid, land, levels)
    even_lon = lax.rem(lax.axis_index("lon"), 2) == 0
    lat = lax.axis_index("lat")
    even_lat = lax.rem(lat, 2) == 0
    lane = lanes()
    from_left = ((lane - 28) >> 2) & 7
    high = (lane & 31) >= 16
    right_part = ((lane + 8) & 31) < 16
    for g in range(ROWS // 8):
        left = [jnp.where(even_lon, rb_ref[i, g], ra_ref[i, g]) for i in range(2)]
        right = [jnp.where(even_lon, ra_ref[i, g], rb_ref[i, g]) for i in range(2)]
        for r in range(8):
            y = 8 * g + r
            for i, own in enumerate(row_edges(refs, y)):
                other = roll_x(jnp.where(from_left == r, left[i], right[i]), -4 * r)
                edge_ref[y, i] = jnp.where(
                    right_part,
                    jnp.where(high, own, other),
                    roll_x(jnp.where(high, other, own), 16),
                )
    for j in range(HALO):
        for ref, at_top in ((a_ref, even_lat), (b_ref, jnp.logical_not(even_lat))):
            y = jnp.where(at_top, ROWS - 1 - j, j)
            for t in range(NT):
                ref[8 * j + t] = load_tracer(tracers, t, y)
            ref[8 * j + 4] = edge_ref[y, 0]
            ref[8 * j + 5] = edge_ref[y, 1]
            ref[8 * j + 6] = load_wet(land, levels, y)
            if j < 3:
                ref[8 * j + 7] = load_row(merid, y)
            if j < 2:
                ref[31 + j] = load_row(zonal, y)

    @pl.when(lat == lax.axis_size("lat") - 1)
    def _():
        flip = COLS - 1 - lane
        flip_edge = (64 * (((lane - 24) >> 5) & 3) + 79 - lane) & (COLS - 1)
        slot = ((lane - 24) >> 5) & 3
        sign = jnp.where(slot < 2, -1.0, 1.0)

        def flipped(p, index):
            return jnp.take_along_axis(b_ref[p], index, axis=1)

        for j in range(HALO):
            for t in range(NT):
                b_ref[8 * j + t] = flipped(8 * j + t, flip)
            b_ref[8 * j + 4] = flipped(8 * j + 4, flip_edge)
            b_ref[8 * j + 5] = flipped(8 * j + 5, flip_edge) * sign
            b_ref[8 * j + 6] = flipped(8 * j + 6, flip)
            if j < 3:
                b_ref[8 * j + 7] = -flipped(8 * j + 7, flip)
            if j < 2:
                b_ref[31 + j] = -flipped(31 + j, flip)


def spread(static):
    slot = ((lanes() - 24) >> 5) & 3
    out = []
    for s in range(3):
        v = jnp.where(slot == s, static, 0.0)
        v = v + roll_x(v, 32)
        out.append(v + roll_x(v, 64))
    return out


def derive(now, above):
    zonal, merid, wet = now
    _, merid_up, wet_up = above
    face_x = wet * roll_x(wet, -1)
    flow_x = 0.5 * (zonal + roll_x(zonal, -1)) * face_x
    face_y = wet * wet_up
    flow_y = 0.5 * (merid + merid_up) * face_y
    face_z = jnp.where(levels_iota() < KZ - 1, wet * roll_k(wet, -1), 0.0)
    grow = UPSTREAM / DIFF_H
    return (
        DIFF_H * face_x,
        0.5 * flow_x,
        grow * flow_x,
        DIFF_H * face_y,
        0.5 * flow_y,
        grow * flow_y,
        DIFF_V * face_z,
        wet,
    )


FX, UX, GX, FY, UY, GY, FZ, WET = range(8)


def advance_rows(src, stat, first, last, put, block, unroll=1):
    def field(y, s, f):
        return stat[y + HALO, int(s == NT), f]

    def face(flow, grow, low, high, before, after, gradient):
        return flow * (low + high) - grow * jnp.where(flow > 0, before, after) - gradient

    start = []
    for s in range(NT + 1):
        c = [src[first + HALO + d, s] for d in (-2, -1, 0, 1)]
        g = [(c[d + 1] - c[d]) * field(first - 2 + d, s, FY) for d in range(3)]
        d0 = g[2] - g[1]
        below = face(
            field(first - 1, s, UY), field(first - 1, s, GY), c[1], c[2], g[1] - g[0], d0, g[1]
        )
        start.append((c[2], c[3], g[2], d0, below))

    def body(i, carry):
        y0 = first + i * block
        stats = [[[field(y0 + r, s, f) for f in range(8)] for r in range(block)] for s in (0, NT)]
        face_up = [[field(y0 + r + 1, s, FY) for r in range(block)] for s in (0, NT)]
        ahead = [[src[y0 + r + 2 + HALO, s] for s in range(NT + 1)] for r in range(block)]
        rows = []
        for r in range(block):
            out, values = [], []
            for s in range(NT + 1):
                e = int(s == NT)
                st = stats[e][r]
                c0, c1, g0, d0, below = carry[s]
                c2 = ahead[r][s]
                g1 = (c2 - c1) * face_up[e][r]
                d1 = g1 - g0
                above = face(st[UY], st[GY], c0, c1, d0, d1, g0)
                cx = roll_x(c0, -1)
                gx = (cx - c0) * st[FX]
                dx = gx - roll_x(gx, 1)
                fx = face(st[UX], st[GX], c0, cx, dx, roll_x(dx, -1), gx)
                gz = (roll_k(c0, -1) - c0) * st[FZ]
                total = c0 + (roll_x(fx, 1) - fx) + (below - above) + (gz - roll_k(gz, 1))
                values.append(st[WET] * total)
                out.append((c1, c2, g1, d1, above))
            carry = out
            rows.append(values)
        for r in range(block):
            put(y0 + r, rows[r])
        return tuple(carry)

    lax.fori_loop(0, (last - first) // block, body, tuple(start), unroll=unroll)


def steps_kernel(
    tracers, zonal, merid, land, levels, edge_ref, ra_ref, rb_ref, out_ref, c0, c1, raw, stat
):
    even_lat = lax.rem(lax.axis_index("lat"), 2) == 0
    lane = lanes()
    zero = jnp.zeros(VREG, jnp.float32)

    def own(y, _):
        for t in range(NT):
            c0[y + HALO, t] = load_tracer(tracers, t, y)
        c0[y + HALO, NT] = edge_ref[y, 0]
        now = (load_row(zonal, y), load_row(merid, y), load_wet(land, levels, y))
        for i, v in enumerate(now):
            raw[y + HALO, 0, i] = v
        for i, v in enumerate(spread(edge_ref[y, 1])):
            raw[y + HALO, 1, i] = v
        return 0

    lax.fori_loop(0, ROWS, own, 0, unroll=4)
    for j in range(HALO):
        for ref, north in ((ra_ref, even_lat), (rb_ref, jnp.logical_not(even_lat))):
            y = jnp.where(north, ROWS + j, -1 - j) + HALO
            for s in range(NT + 1):
                c0[y, s] = ref[8 * j + s]
            raw[y, 0, 0] = ref[31 + j] if j < 2 else zero
            raw[y, 0, 1] = ref[8 * j + 7] if j < 3 else zero
            raw[y, 0, 2] = ref[8 * j + 6]
            for i, v in enumerate(spread(ref[8 * j + 5])):
                raw[y, 1, i] = v

    def statics(y, _):
        for e in range(2):
            now = [raw[y, e, i] for i in range(3)]
            above = [raw[y + 1, e, i] for i in range(3)]
            for f, v in enumerate(derive(now, above)):
                stat[y, e, f] = v
        return 0

    lax.fori_loop(0, EXT - 1, statics, 0, unroll=3)

    def keep(y, values):
        for s, v in enumerate(values):
            c1[y + HALO, s] = v

    advance_rows(c0, stat, -2, ROWS + 2, keep, 4)
    near = (lane < 4) | (lane >= COLS - 4)
    high = (lane & 31) >= 16

    def finish(y, values):
        edge = jnp.where(high, values[NT], roll_x(values[NT], -16))
        for t in range(NT):
            out_ref[t, pl.ds(y, KZ, stride=ROWS), :] = jnp.where(
                near, roll_x(edge, -32 * (t + 1)), values[t]
            )

    advance_rows(c1, stat, 0, ROWS, finish, 4)


def neighbour_swaps(size, odd, wrap):
    pairs = []
    for i in range(size):
        j = i + 1 if i % 2 == int(odd) else i - 1
        if wrap or 0 <= j < size:
            pairs.append((i, j % size))
    return pairs


def per_device(tracers, zonal, merid, land, levels):
    n_lon, n_lat = lax.axis_size("lon"), lax.axis_size("lat")
    f32 = jnp.float32
    args = (
        tracers.reshape(NT, KZ * ROWS, COLS),
        zonal.reshape(KZ * ROWS, COLS),
        merid.reshape(KZ * ROWS, COLS),
        land,
        levels,
    )
    lon_pack = jax.ShapeDtypeStruct((2, ROWS // 8) + VREG, f32)
    lat_pack = jax.ShapeDtypeStruct((PAYLOAD,) + VREG, f32)

    with jax.named_scope("pack_lon"):
        la, lb = pl.pallas_call(pack_lon_kernel, out_shape=(lon_pack, lon_pack))(*args)
    with jax.named_scope("swap_lon"):
        ra = lax.ppermute(la, "lon", neighbour_swaps(n_lon, False, True))
        rb = lax.ppermute(lb, "lon", neighbour_swaps(n_lon, True, True))
    with jax.named_scope("pack_lat"):
        edges = jax.ShapeDtypeStruct((ROWS, 2) + VREG, f32)
        ma, mb, edge = pl.pallas_call(
            pack_lat_kernel, out_shape=(lat_pack, lat_pack, edges)
        )(*args, ra, rb)
    with jax.named_scope("swap_lat"):
        sa = lax.ppermute(ma, "lat", neighbour_swaps(n_lat, False, False))
        pairs = [
            (lon * n_lat + i, lon * n_lat + j)
            for lon in range(n_lon)
            for i, j in neighbour_swaps(n_lat, True, False)
        ]
        pairs += [
            (lon * n_lat + n_lat - 1, (n_lon - 1 - lon) * n_lat + n_lat - 1)
            for lon in range(n_lon)
        ]
        sb = lax.ppermute(mb, ("lon", "lat"), pairs)
    with jax.named_scope("two_steps"):
        out = pl.pallas_call(
            steps_kernel,
            out_shape=jax.ShapeDtypeStruct((NT, KZ * ROWS, COLS), f32),
            scratch_shapes=[
                pltpu.VMEM((EXT, NT + 1) + VREG, f32),
                pltpu.VMEM((EXT, NT + 1) + VREG, f32),
                pltpu.VMEM((EXT, 2, 3) + VREG, f32),
                pltpu.VMEM((EXT, 2, 8) + VREG, f32),
            ],
        )(*args, edge, sa, sb)
    return out.reshape(tracers.shape)


def solution(mesh):
    return jax.shard_map(
        per_device,
        mesh=mesh,
        in_specs=(
            P(None, None, "lat", "lon"),
            P(None, "lat", "lon"),
            P(None, "lat", "lon"),
            P("lat", "lon"),
            P("lat", "lon"),
        ),
        out_specs=P(None, None, "lat", "lon"),
        check_vma=False,
    )
```

```python
import jax
import jax.numpy as jnp
from jax import lax
from jax.experimental import pallas as pl
from jax.experimental.pallas import tpu as pltpu
from jax.sharding import PartitionSpec as P


KZ = 8
ROWS = 32
COLS = 128
NT = 4
HALO = 4
EXT = ROWS + 2 * HALO
PAYLOAD = 25
MERID_AT = 20
ZONAL_AT = 23
FIELDS = 10
VMEM_LIMIT = 12 * 2**20

DIFF_H = 0.1
DIFF_V = 0.2
UPSTREAM = 1.0 / 6.0

VREG = (KZ, COLS)


def lanes():
    return lax.broadcasted_iota(jnp.int32, VREG, 1)


def levels_iota():
    return lax.broadcasted_iota(jnp.int32, VREG, 0)


def roll_x(v, shift):
    shift %= COLS
    return v if shift == 0 else pltpu.roll(v, shift, 1)


def roll_k(v, shift):
    return pltpu.roll(v, shift % KZ, 0)


def load_row(ref, y):
    return ref[pl.ds(y, KZ, stride=ROWS), :]


def load_tracer(ref, t, y):
    return ref[t, pl.ds(y, KZ, stride=ROWS), :]


def load_wet(land_ref, levels_ref, y):
    depth = jnp.where(land_ref[pl.ds(y, 1), :] == 1, levels_ref[pl.ds(y, 1), :], 0)
    return jnp.where(levels_iota() < jnp.broadcast_to(depth, VREG), 1.0, 0.0)


def halo_row(r):
    return -1 - r if r < HALO else ROWS + r - HALO


def gather_edges(parts):
    slot = ((lanes() - 16) >> 5) & 3
    out = roll_x(parts[-1], 32 * len(parts))
    for t in range(len(parts) - 1):
        out = jnp.where(slot == t, roll_x(parts[t], 32 * (t + 1)), out)
    return out


def pick(v, index):
    return jnp.take_along_axis(v, index, axis=1)


def edge_index(slot, r=0):
    lane = lanes()
    at = (lane - 24) & 31
    field = ((lane - 24) & 96) if slot is None else 32 * slot
    return (field + 4 * r + jnp.where(at < 16, at + 24, at + 8)) & (COLS - 1)


def edge_fields(moving, static, r=0):
    out = [pick(moving, edge_index(None, r))]
    return out + [pick(static, edge_index(f, r)) for f in range(3)]


def pack_eight(rows):
    lane = lanes()
    to_right = ((lane - 28) >> 2) & 7
    to_left = (lane >> 2) & 7
    right = left = rows[0]
    for r in range(1, 8):
        moved = roll_x(rows[r], 4 * r)
        right = jnp.where(to_right == r, moved, right)
        left = jnp.where(to_left == r, moved, left)
    return right, left


def is_even(axis):
    return lax.rem(lax.axis_index(axis), 2) == 0


def pack_lat_kernel(tracers, zonal, merid, land, levels, a_ref, b_ref):
    even = is_even("lat")
    for j in range(HALO):
        for ref, at_top in ((a_ref, even), (b_ref, jnp.logical_not(even))):
            y = jnp.where(at_top, ROWS - 1 - j, j)
            for t in range(NT):
                ref[5 * j + t] = load_tracer(tracers, t, y)
            ref[5 * j + 4] = load_wet(land, levels, y)
            if j < 3:
                ref[MERID_AT + j] = load_row(merid, y)
            if j < 2:
                ref[ZONAL_AT + j] = load_row(zonal, y)

    @pl.when(lax.axis_index("lat") == lax.axis_size("lat") - 1)
    def _():
        flip = COLS - 1 - lanes()
        for p in range(PAYLOAD):
            v = pick(b_ref[p], flip)
            b_ref[p] = v if p < MERID_AT else -v


def own_kernel(
    tracers, zonal, merid, land, levels, c_ref, q_ref, edge_ref, a_ref, b_ref
):
    even = is_even("lon")
    for g in range(ROWS // 8):
        moving, static = [], []
        for r in range(8):
            y = 8 * g + r
            cs = [load_tracer(tracers, t, y) for t in range(NT)]
            qs = [load_row(zonal, y), load_row(merid, y), load_wet(land, levels, y)]
            for t in range(NT):
                c_ref[y, t] = cs[t]
            for f in range(3):
                q_ref[y, f] = qs[f]
            moving.append(gather_edges(cs))
            static.append(gather_edges(qs))
        for i, rows in enumerate((moving, static)):
            right, left = pack_eight(rows)
            a_ref[i, g] = jnp.where(even, right, left)
            b_ref[i, g] = jnp.where(even, left, right)
        for r in range(8):
            for i, v in enumerate(edge_fields(moving[r], static[r])):
                edge_ref[8 * g + r, i] = v


def pack_lon_kernel(
    ra_ref, rb_ref, pa_ref, pb_ref, a_ref, b_ref, c_ref, q_ref, static_ref, moving_ref
):
    even_lon = is_even("lon")
    even_lat = is_even("lat")
    bottom = lax.axis_index("lat") == 0
    moving, static = [], []
    for r in range(8):
        j = r % HALO

        def get(p):
            north, south = (ra_ref, rb_ref) if r >= HALO else (rb_ref, ra_ref)
            v = jnp.where(even_lat, north[p], south[p])
            return v if r >= HALO else jnp.where(bottom, 0.0, v)

        cs = [get(5 * j + t) for t in range(NT)]
        zero = jnp.zeros(VREG, jnp.float32)
        qs = [
            get(ZONAL_AT + j) if j < 2 else zero,
            get(MERID_AT + j) if j < 3 else zero,
            get(5 * j + 4),
        ]
        for t in range(NT):
            c_ref[r, t] = cs[t]
        for f in range(3):
            q_ref[r, f] = qs[f]
        moving.append(gather_edges(cs))
        static.append(gather_edges(qs))
        moving_ref[r] = moving[r]
        static_ref[r] = static[r]
    for i, rows in enumerate((moving, static)):
        right, left = pack_eight(rows)
        a_ref[i, ROWS // 8] = jnp.where(even_lon, right, left)
        b_ref[i, ROWS // 8] = jnp.where(even_lon, left, right)
        for g in range(ROWS // 8):
            a_ref[i, g] = pa_ref[i, g]
            b_ref[i, g] = pb_ref[i, g]


def derive_along(flow, face, face_before, face_after):
    up = jnp.maximum(flow, 0.0) * (UPSTREAM / 2)
    down = jnp.minimum(flow, 0.0) * (UPSTREAM / 2)
    near = (up - down) + DIFF_H * face
    mean = 0.25 * flow
    far_before, far_after = up * face_before, down * face_after
    return mean + near + far_before, mean - near + far_after, far_before, far_after


def derive(zonal, merid, wet):
    here = wet[1]
    face = here * roll_x(here, -1)
    flow = (zonal + roll_x(zonal, -1)) * face
    along_x = derive_along(flow, face, roll_x(face, 1), roll_x(face, -1))
    faces = [wet[d] * wet[d + 1] for d in range(3)]
    flow = (merid[0] + merid[1]) * faces[1]
    along_y = derive_along(flow, faces[1], faces[0], faces[2])
    face_z = jnp.where(levels_iota() < KZ - 1, here * roll_k(here, -1), 0.0)
    return along_x + along_y + (DIFF_V * face_z, here)


X, Y, FZ, WET = 0, 4, 8, 9


def statics(raw, stat, block):
    def body(i, _):
        y = 1 + i * block
        merid = [raw[y, 1]]
        wet = [raw[y + d, 2] for d in range(-1, 2)]
        rows = []
        for d in range(block):
            merid = merid[-1:] + [raw[y + d + 1, 1]]
            wet = wet[-3:] + [raw[y + d + 2, 2]]
            rows.append(derive(raw[y + d, 0], merid, wet))
        for d in range(block):
            for f in range(FIELDS):
                stat[y + d, f] = rows[d][f]
        return 0

    lax.fori_loop(0, (EXT - 3) // block, body, 0)
    for d in range((EXT - 3) % block):
        y = EXT - 3 - d
        row = derive(
            raw[y, 0], [raw[y, 1], raw[y + 1, 1]], [raw[y + e, 2] for e in range(-1, 3)]
        )
        for f in range(FIELDS):
            stat[y, f] = row[f]


def flux(st, at, before, low, high, after):
    return (st[at] * low + st[at + 1] * high) - (st[at + 2] * before + st[at + 3] * after)


def advance_rows(src, stat, streams, first, last, block, put):
    def body(i, _):
        y = first + HALO + i * block
        c = [[src[y + d, s] for s in range(streams)] for d in range(-2, 2)]
        st = [stat[y - 1, f] for f in range(Y + 4)]
        below = [flux(st, Y, c[0][s], c[1][s], c[2][s], c[3][s]) for s in range(streams)]
        rows = []
        for d in range(block):
            st = [stat[y + d, f] for f in range(FIELDS)]
            c = c[1:] + [[src[y + d + 2, s] for s in range(streams)]]
            values = []
            for s in range(streams):
                here = c[1][s]
                above = flux(st, Y, c[0][s], here, c[2][s], c[3][s])
                east = flux(
                    st, X, roll_x(here, 1), here, roll_x(here, -1), roll_x(here, -2)
                )
                gz = (roll_k(here, -1) - here) * st[FZ]
                total = (here + (roll_x(east, 1) - east)) + (below[s] - above)
                values.append(st[WET] * (total + (gz - roll_k(gz, 1))))
                below[s] = above
            rows.append(values)
        for d in range(block):
            put(y - HALO + d, rows[d])
        return 0

    lax.fori_loop(0, (last - first) // block, body, 0)


def main_kernel(c_ref, q_ref, ch_ref, qh_ref, out_ref, c0, c1, raw, stat):
    for r in range(8):
        y = halo_row(r) + HALO
        for t in range(NT):
            c0[y, t] = ch_ref[r, t]
        for f in range(3):
            raw[y, f] = qh_ref[r, f]

    def own(y, _):
        for t in range(NT):
            c0[y + HALO, t] = c_ref[y, t]
        for f in range(3):
            raw[y + HALO, f] = q_ref[y, f]
        return 0

    lax.fori_loop(0, ROWS, own, 0, unroll=8)
    statics(raw, stat, 12)

    def keep(y, values):
        for t in range(NT):
            c1[y + HALO, t] = values[t]

    advance_rows(c0, stat, NT, -2, ROWS + 2, MAIN_BLOCK_1, keep)

    def finish(y, values):
        for t in range(NT):
            out_ref[t, pl.ds(y, KZ, stride=ROWS), :] = values[t]

    advance_rows(c1, stat, NT, 0, ROWS, MAIN_BLOCK_2, finish)


MAIN_BLOCK_1 = 9
MAIN_BLOCK_2 = 8
EDGE_BLOCK_1 = 18
EDGE_BLOCK_2 = 16


def edge_kernel(
    main_ref, edge_ref, mh_ref, sh_ref, ra_ref, rb_ref, out_ref, e0, e1, raw, stat, native
):
    even = is_even("lon")
    lane = lanes()
    from_left = ((lane - 28) >> 2) & 7
    at = (lane - 24) & 31
    own = (at < 8) | (at >= 24)
    for g in range(ROWS // 8 + 1):
        left = [jnp.where(even, rb_ref[i, g], ra_ref[i, g]) for i in range(2)]
        right = [jnp.where(even, ra_ref[i, g], rb_ref[i, g]) for i in range(2)]
        for r in range(8):
            both = [jnp.where(from_left == r, left[i], right[i]) for i in range(2)]
            other = edge_fields(*both, r)
            if g < ROWS // 8:
                y = 8 * g + r
                mine = [edge_ref[y, i] for i in range(4)]
            else:
                y = halo_row(r)
                mine = edge_fields(mh_ref[r], sh_ref[r])
            row = [jnp.where(own, m, o) for m, o in zip(mine, other)]
            e0[y + HALO, 0] = row[0]
            for f in range(3):
                raw[y + HALO, f] = row[f + 1]
    statics(raw, stat, 18)

    def keep(y, values):
        e1[y + HALO, 0] = values[0]

    advance_rows(e0, stat, 1, -2, ROWS + 2, EDGE_BLOCK_1, keep)
    high = (lane & 31) >= 16

    def finish(y, values):
        native[pl.ds(y, KZ, stride=ROWS), :] = jnp.where(
            high, values[0], roll_x(values[0], -16)
        )

    advance_rows(e1, stat, 1, 0, ROWS, EDGE_BLOCK_2, finish)
    near = (lane < 4) | (lane >= COLS - 4)
    for i in range(KZ * ROWS // 8):
        edge = native[8 * i : 8 * i + 8, :]
        for t in range(NT):
            out_ref[t, 8 * i : 8 * i + 8, :] = jnp.where(
                near, roll_x(edge, -32 * (t + 1)), main_ref[t, 8 * i : 8 * i + 8, :]
            )


def neighbour_swaps(size, odd, wrap):
    pairs = []
    for i in range(size):
        j = i + 1 if i % 2 == int(odd) else i - 1
        if wrap or 0 <= j < size:
            pairs.append((i, j % size))
    return pairs


def odd_lat_swaps(n_lon, n_lat):
    pairs = []
    for lon in range(n_lon):
        for i, j in neighbour_swaps(n_lat, True, False):
            pairs.append((lon * n_lat + i, lon * n_lat + j))
        pairs.append((lon * n_lat + n_lat - 1, (n_lon - 1 - lon) * n_lat + n_lat - 1))
        pairs.append((lon * n_lat, (lon ^ 1) * n_lat))
    return pairs


def call(kernel, name, outs, scratch, flops, *args):
    f32 = jnp.float32
    nbytes = sum(4 * a.size for a in args)
    with jax.named_scope(name):
        return pl.pallas_call(
            kernel,
            out_shape=tuple(jax.ShapeDtypeStruct(tuple(o) + VREG, f32) for o in outs),
            scratch_shapes=[pltpu.VMEM(tuple(o) + VREG, f32) for o in scratch],
            compiler_params=pltpu.CompilerParams(vmem_limit_bytes=VMEM_LIMIT),
            cost_estimate=pl.CostEstimate(
                flops=flops, bytes_accessed=nbytes, transcendentals=0
            ),
        )(*args)


def per_device(tracers, zonal, merid, land, levels):
    n_lon, n_lat = lax.axis_size("lon"), lax.axis_size("lat")
    f32 = jnp.float32
    args = (
        tracers.reshape(NT, KZ * ROWS, COLS),
        zonal.reshape(KZ * ROWS, COLS),
        merid.reshape(KZ * ROWS, COLS),
        land,
        levels,
    )
    groups = ROWS // 8
    ma, mb = call(pack_lat_kernel, "pack_lat", [(PAYLOAD,)] * 2, [], 10**5, *args)
    with jax.named_scope("swap_lat"):
        sa = lax.ppermute(ma, "lat", neighbour_swaps(n_lat, False, False))
        sb = lax.ppermute(mb, ("lon", "lat"), odd_lat_swaps(n_lon, n_lat))
    c, q, edge, pa, pb = call(
        own_kernel,
        "own_edges",
        [(ROWS, NT), (ROWS, 3), (ROWS, 4), (2, groups), (2, groups)],
        [],
        10**6,
        *args,
    )
    la, lb, ch, qh, sh, mh = call(
        pack_lon_kernel,
        "pack_lon",
        [(2, groups + 1), (2, groups + 1), (8, NT), (8, 3), (8,), (8,)],
        [],
        10**5,
        sa,
        sb,
        pa,
        pb,
    )
    with jax.named_scope("swap_lon"):
        ta = lax.ppermute(la, "lon", neighbour_swaps(n_lon, False, True))
        tb = lax.ppermute(lb, "lon", neighbour_swaps(n_lon, True, True))
    with jax.named_scope("main"):
        main = pl.pallas_call(
            main_kernel,
            out_shape=jax.ShapeDtypeStruct((NT, KZ * ROWS, COLS), f32),
            scratch_shapes=[
                pltpu.VMEM((EXT, NT) + VREG, f32),
                pltpu.VMEM((EXT, NT) + VREG, f32),
                pltpu.VMEM((EXT, 3) + VREG, f32),
                pltpu.VMEM((EXT, FIELDS) + VREG, f32),
            ],
            compiler_params=pltpu.CompilerParams(vmem_limit_bytes=VMEM_LIMIT),
            cost_estimate=pl.CostEstimate(
                flops=10**7, bytes_accessed=2 * 10**6, transcendentals=0
            ),
        )(c, q, ch, qh)
    with jax.named_scope("edges"):
        out = pl.pallas_call(
            edge_kernel,
            out_shape=jax.ShapeDtypeStruct((NT, KZ * ROWS, COLS), f32),
            scratch_shapes=[
                pltpu.VMEM((EXT, 1) + VREG, f32),
                pltpu.VMEM((EXT, 1) + VREG, f32),
                pltpu.VMEM((EXT, 3) + VREG, f32),
                pltpu.VMEM((EXT, FIELDS) + VREG, f32),
                pltpu.VMEM((KZ * ROWS, COLS), f32),
            ],
            compiler_params=pltpu.CompilerParams(vmem_limit_bytes=VMEM_LIMIT),
            cost_estimate=pl.CostEstimate(
                flops=10**6, bytes_accessed=10**6, transcendentals=0
            ),
        )(main, edge, mh, sh, ta, tb)
    return out.reshape(tracers.shape)


def solution(mesh):
    return jax.shard_map(
        per_device,
        mesh=mesh,
        in_specs=(
            P(None, None, "lat", "lon"),
            P(None, "lat", "lon"),
            P(None, "lat", "lon"),
            P("lat", "lon"),
            P("lat", "lon"),
        ),
        out_specs=P(None, None, "lat", "lon"),
        check_vma=False,
    )
```

```python
import jax
import jax.numpy as jnp
from jax import lax
from jax.experimental import pallas as pl
from jax.experimental.pallas import tpu as pltpu
from jax.sharding import PartitionSpec as P


KZ = 8
ROWS = 32
COLS = 128
NT = 4
HALO = 4
EXT = ROWS + 2 * HALO
PAYLOAD = 25
MERID_AT = 20
ZONAL_AT = 23
FIELDS = 10
VMEM_LIMIT = 12 * 2**20

DIFF_H = 0.1
DIFF_V = 0.2
UPSTREAM = 1.0 / 6.0

VREG = (KZ, COLS)


def lanes():
    return lax.broadcasted_iota(jnp.int32, VREG, 1)


def levels_iota():
    return lax.broadcasted_iota(jnp.int32, VREG, 0)


def roll_x(v, shift):
    shift %= COLS
    return v if shift == 0 else pltpu.roll(v, shift, 1)


def roll_k(v, shift):
    return pltpu.roll(v, shift % KZ, 0)


def load_row(ref, y):
    return ref[pl.ds(y, KZ, stride=ROWS), :]


def load_tracer(ref, t, y):
    return ref[t, pl.ds(y, KZ, stride=ROWS), :]


def load_wet(land_ref, levels_ref, y):
    depth = jnp.where(land_ref[pl.ds(y, 1), :] == 1, levels_ref[pl.ds(y, 1), :], 0)
    return jnp.where(levels_iota() < jnp.broadcast_to(depth, VREG), 1.0, 0.0)


def halo_row(r):
    return -1 - r if r < HALO else ROWS + r - HALO


def gather_edges(parts):
    slot = ((lanes() - 16) >> 5) & 3
    out = roll_x(parts[-1], 32 * len(parts))
    for t in range(len(parts) - 1):
        out = jnp.where(slot == t, roll_x(parts[t], 32 * (t + 1)), out)
    return out


def pick(v, index):
    return jnp.take_along_axis(v, index, axis=1)


def edge_index(slot, r=0):
    lane = lanes()
    at = (lane - 24) & 31
    field = ((lane - 24) & 96) if slot is None else 32 * slot
    return (field + 4 * r + jnp.where(at < 16, at + 24, at + 8)) & (COLS - 1)


def edge_fields(moving, static, r=0):
    out = [pick(moving, edge_index(None, r))]
    return out + [pick(static, edge_index(f, r)) for f in range(3)]


def pack_eight(rows):
    lane = lanes()
    to_right = ((lane - 28) >> 2) & 7
    to_left = (lane >> 2) & 7
    right = left = rows[0]
    for r in range(1, 8):
        moved = roll_x(rows[r], 4 * r)
        right = jnp.where(to_right == r, moved, right)
        left = jnp.where(to_left == r, moved, left)
    return right, left


def is_even(axis):
    return lax.rem(lax.axis_index(axis), 2) == 0


def pack_lat_kernel(
    tracers, zonal, merid, land, levels, a_ref, b_ref, c_rows, z_rows, m_rows, d_rows, sems
):
    copies = []

    def fetch(source, target):
        copies.append(pltpu.make_async_copy(source, target, sems.at[len(copies)]))
        copies[-1].start()

    for side, rows in enumerate((pl.ds(0, 8), pl.ds(ROWS - 8, 8))):
        fetch(tracers.at[:, rows, :], c_rows.at[side])
        fetch(zonal.at[:, rows, :], z_rows.at[side])
        fetch(merid.at[:, rows, :], m_rows.at[side])
        fetch(land.at[rows, :], d_rows.at[side, 0])
        fetch(levels.at[rows, :], d_rows.at[side, 1])
    for copy in copies:
        copy.wait()
    even = is_even("lat")
    flat_c = c_rows.reshape(2 * NT, KZ * 8, COLS)
    flat_z, flat_m = z_rows.reshape(2, KZ * 8, COLS), m_rows.reshape(2, KZ * 8, COLS)
    for j in range(HALO):
        for ref, at_top in ((a_ref, even), (b_ref, jnp.logical_not(even))):
            side = jnp.where(at_top, 1, 0)
            y = jnp.where(at_top, 7 - j, j)
            row = pl.ds(y, KZ, stride=8)
            for t in range(NT):
                ref[5 * j + t] = flat_c[side * NT + t, row, :]
            depth = jnp.where(
                d_rows[side, 0, pl.ds(y, 1), :] == 1, d_rows[side, 1, pl.ds(y, 1), :], 0
            )
            ref[5 * j + 4] = jnp.where(
                levels_iota() < jnp.broadcast_to(depth, VREG), 1.0, 0.0
            )
            if j < 3:
                ref[MERID_AT + j] = flat_m[side, row, :]
            if j < 2:
                ref[ZONAL_AT + j] = flat_z[side, row, :]

    @pl.when(lax.axis_index("lat") == lax.axis_size("lat") - 1)
    def _():
        flip = COLS - 1 - lanes()
        for p in range(PAYLOAD):
            v = pick(b_ref[p], flip)
            b_ref[p] = v if p < MERID_AT else -v


def own_kernel(*refs):
    sources, (c0, c1, raw, stat, main_ref, edge_ref, a_ref, b_ref) = refs[:5], refs[5:13]
    targets, sems = refs[13:18], refs[18]
    copies = [
        pltpu.make_async_copy(a, b, sems.at[i])
        for i, (a, b) in enumerate(zip(sources, targets))
    ]
    for copy in copies:
        copy.start()
    for copy in copies:
        copy.wait()
    tracers, zonal, merid, land, levels = targets
    even = is_even("lon")
    for g in range(ROWS // 8):
        moving, static = [], []
        for r in range(8):
            y = 8 * g + r
            cs = [load_tracer(tracers, t, y) for t in range(NT)]
            qs = [load_row(zonal, y), load_row(merid, y), load_wet(land, levels, y)]
            for t in range(NT):
                c0[y + HALO, t] = cs[t]
            for f in range(3):
                raw[y + HALO, f] = qs[f]
            moving.append(gather_edges(cs))
            static.append(gather_edges(qs))
        for i, rows in enumerate((moving, static)):
            right, left = pack_eight(rows)
            a_ref[i, g] = jnp.where(even, right, left)
            b_ref[i, g] = jnp.where(even, left, right)
        for r in range(8):
            for i, v in enumerate(edge_fields(moving[r], static[r])):
                edge_ref[8 * g + r, i] = v
    statics(raw, stat, 1, ROWS - 2, 10)
    advance_rows(c0, stat, NT, 2, ROWS - 2, 7, keep_in(c1))
    advance_rows(c1, stat, NT, 4, ROWS - 4, 8, native_in(main_ref))


def pack_lon_kernel(
    ra_ref, rb_ref, pa_ref, pb_ref, a_ref, b_ref, c_ref, q_ref, static_ref, moving_ref
):
    even_lon = is_even("lon")
    even_lat = is_even("lat")
    bottom = lax.axis_index("lat") == 0
    moving, static = [], []
    for r in range(8):
        j = r % HALO

        def get(p):
            north, south = (ra_ref, rb_ref) if r >= HALO else (rb_ref, ra_ref)
            v = jnp.where(even_lat, north[p], south[p])
            return v if r >= HALO else jnp.where(bottom, 0.0, v)

        cs = [get(5 * j + t) for t in range(NT)]
        zero = jnp.zeros(VREG, jnp.float32)
        qs = [
            get(ZONAL_AT + j) if j < 2 else zero,
            get(MERID_AT + j) if j < 3 else zero,
            get(5 * j + 4),
        ]
        for t in range(NT):
            c_ref[r, t] = cs[t]
        for f in range(3):
            q_ref[r, f] = qs[f]
        moving.append(gather_edges(cs))
        static.append(gather_edges(qs))
        moving_ref[r] = moving[r]
        static_ref[r] = static[r]
    for i, rows in enumerate((moving, static)):
        right, left = pack_eight(rows)
        a_ref[i, ROWS // 8] = jnp.where(even_lon, right, left)
        b_ref[i, ROWS // 8] = jnp.where(even_lon, left, right)
        for g in range(ROWS // 8):
            a_ref[i, g] = pa_ref[i, g]
            b_ref[i, g] = pb_ref[i, g]


def derive_along(flow, face, face_before, face_after):
    up = jnp.maximum(flow, 0.0) * (UPSTREAM / 2)
    down = jnp.minimum(flow, 0.0) * (UPSTREAM / 2)
    near = (up - down) + DIFF_H * face
    mean = 0.25 * flow
    far_before, far_after = up * face_before, down * face_after
    return mean + near + far_before, mean - near + far_after, far_before, far_after


def derive(zonal, merid, wet):
    here = wet[1]
    face = here * roll_x(here, -1)
    flow = (zonal + roll_x(zonal, -1)) * face
    along_x = derive_along(flow, face, roll_x(face, 1), roll_x(face, -1))
    faces = [wet[d] * wet[d + 1] for d in range(3)]
    flow = (merid[0] + merid[1]) * faces[1]
    along_y = derive_along(flow, faces[1], faces[0], faces[2])
    face_z = jnp.where(levels_iota() < KZ - 1, here * roll_k(here, -1), 0.0)
    return along_x + along_y + (DIFF_V * face_z, here)


X, Y, FZ, WET = 0, 4, 8, 9


def statics_block(raw, stat, y, block):
    merid = [raw[y, 1]]
    wet = [raw[y + d, 2] for d in range(-1, 2)]
    rows = []
    for d in range(block):
        merid = merid[-1:] + [raw[y + d + 1, 1]]
        wet = wet[-3:] + [raw[y + d + 2, 2]]
        rows.append(derive(raw[y + d, 0], merid, wet))

    def store():
        for d in range(block):
            for f in range(FIELDS):
                stat[y + d, f] = rows[d][f]

    return store


def statics(raw, stat, first, last, block):
    def body(i, _):
        statics_block(raw, stat, first + HALO + i * block, block)()
        return 0

    count = (last - first) // block
    lax.fori_loop(0, count, body, 0)
    rest = last - first - count * block
    if rest:
        statics_block(raw, stat, last + HALO - rest, rest)()


def flux(st, at, before, low, high, after):
    return (st[at] * low + st[at + 1] * high) - (st[at + 2] * before + st[at + 3] * after)


def advance_block(src, stat, streams, y, block):
    c = [[src[y + d, s] for s in range(streams)] for d in range(-2, 2)]
    st = [stat[y - 1, f] for f in range(Y + 4)]
    below = [flux(st, Y, c[0][s], c[1][s], c[2][s], c[3][s]) for s in range(streams)]
    rows = []
    for d in range(block):
        st = [stat[y + d, f] for f in range(FIELDS)]
        c = c[1:] + [[src[y + d + 2, s] for s in range(streams)]]
        values = []
        for s in range(streams):
            here = c[1][s]
            above = flux(st, Y, c[0][s], here, c[2][s], c[3][s])
            east = flux(st, X, roll_x(here, 1), here, roll_x(here, -1), roll_x(here, -2))
            gz = (roll_k(here, -1) - here) * st[FZ]
            total = (here + (roll_x(east, 1) - east)) + (below[s] - above)
            values.append(st[WET] * (total + (gz - roll_k(gz, 1))))
            below[s] = above
        rows.append(values)
    return rows


def advance_rows(src, stat, streams, first, last, block, put):
    def body(i, _):
        y = first + i * block
        for d, values in enumerate(advance_block(src, stat, streams, y + HALO, block)):
            put(y + d, values)
        return 0

    assert (last - first) % block == 0
    lax.fori_loop(0, (last - first) // block, body, 0)


def keep_in(ref):
    def put(y, values):
        for s, v in enumerate(values):
            ref[y + HALO, s] = v

    return put


def native_in(ref):
    def put(y, values):
        for t, v in enumerate(values):
            ref[t, pl.ds(y, KZ, stride=ROWS), :] = v

    return put


def border_kernel(
    _c0, _c1, _raw, _stat, _main, ch_ref, qh_ref, mh_ref, sh_ref, c0, c1, raw, stat, main_ref, eh_ref
):
    for r in range(8):
        y = halo_row(r) + HALO
        for t in range(NT):
            c0[y, t] = ch_ref[r, t]
        for f in range(3):
            raw[y, f] = qh_ref[r, f]
    for store in [statics_block(raw, stat, y + HALO, 4) for y in (-3, ROWS - 2)]:
        store()
    for step, src, firsts, put in (
        (0, c0, (-2, ROWS - 2), keep_in(c1)),
        (1, c1, (0, ROWS - 4), native_in(main_ref)),
    ):
        done = [(y, advance_block(src, stat, NT, y + HALO, 4)) for y in firsts]
        for y, rows in done:
            for d, values in enumerate(rows):
                put(y + d, values)
    for r in range(8):
        for i, v in enumerate(edge_fields(mh_ref[r], sh_ref[r])):
            eh_ref[r, i] = v


EDGE_BLOCK_1 = 18
EDGE_BLOCK_2 = 16


def edge_kernel(
    main_ref, edge_ref, eh_ref, ra_ref, rb_ref, out_ref, e0, e1, raw, stat, native
):
    even = is_even("lon")
    lane = lanes()
    from_left = ((lane - 28) >> 2) & 7
    at = (lane - 24) & 31
    own = (at < 8) | (at >= 24)
    for g in range(ROWS // 8 + 1):
        left = [jnp.where(even, rb_ref[i, g], ra_ref[i, g]) for i in range(2)]
        right = [jnp.where(even, ra_ref[i, g], rb_ref[i, g]) for i in range(2)]
        for r in range(8):
            both = [jnp.where(from_left == r, left[i], right[i]) for i in range(2)]
            other = edge_fields(*both, r)
            if g < ROWS // 8:
                y = 8 * g + r
                mine = [edge_ref[y, i] for i in range(4)]
            else:
                y = halo_row(r)
                mine = [eh_ref[r, i] for i in range(4)]
            row = [jnp.where(own, m, o) for m, o in zip(mine, other)]
            e0[y + HALO, 0] = row[0]
            for f in range(3):
                raw[y + HALO, f] = row[f + 1]
    statics(raw, stat, -3, ROWS + 2, 18)

    advance_rows(e0, stat, 1, -2, ROWS + 2, EDGE_BLOCK_1, keep_in(e1))
    high = (lane & 31) >= 16

    def finish(y, values):
        native[pl.ds(y, KZ, stride=ROWS), :] = jnp.where(
            high, values[0], roll_x(values[0], -16)
        )

    advance_rows(e1, stat, 1, 0, ROWS, EDGE_BLOCK_2, finish)
    near = (lane < 4) | (lane >= COLS - 4)
    for i in range(KZ * ROWS // 8):
        edge = native[8 * i : 8 * i + 8, :]
        for t in range(NT):
            out_ref[t, 8 * i : 8 * i + 8, :] = jnp.where(
                near, roll_x(edge, -32 * (t + 1)), main_ref[t, 8 * i : 8 * i + 8, :]
            )


def neighbour_swaps(size, odd, wrap):
    pairs = []
    for i in range(size):
        j = i + 1 if i % 2 == int(odd) else i - 1
        if wrap or 0 <= j < size:
            pairs.append((i, j % size))
    return pairs


def odd_lat_swaps(n_lon, n_lat):
    pairs = []
    for lon in range(n_lon):
        for i, j in neighbour_swaps(n_lat, True, False):
            pairs.append((lon * n_lat + i, lon * n_lat + j))
        pairs.append((lon * n_lat + n_lat - 1, (n_lon - 1 - lon) * n_lat + n_lat - 1))
        pairs.append((lon * n_lat, (lon ^ 1) * n_lat))
    return pairs


def call(kernel, name, outs, scratch, flops, *args, aliases={}, in_hbm=False):
    f32 = jnp.float32
    kwargs = {}
    if in_hbm:
        args = [pltpu.with_memory_space_constraint(a, pltpu.HBM) for a in args]
        kwargs = dict(in_specs=[pl.BlockSpec(memory_space=pltpu.HBM)] * len(args))
    with jax.named_scope(name):
        return pl.pallas_call(
            kernel,
            out_shape=tuple(jax.ShapeDtypeStruct(tuple(o), f32) for o in outs),
            scratch_shapes=scratch,
            input_output_aliases=aliases,
            compiler_params=pltpu.CompilerParams(vmem_limit_bytes=VMEM_LIMIT),
            cost_estimate=pl.CostEstimate(
                flops=flops,
                bytes_accessed=sum(4 * a.size for a in args),
                transcendentals=0,
            ),
            **kwargs,
        )(*args)


def per_device(tracers, zonal, merid, land, levels):
    n_lon, n_lat = lax.axis_size("lon"), lax.axis_size("lat")
    f32 = jnp.float32
    flat = (
        tracers.reshape(NT, KZ * ROWS, COLS),
        zonal.reshape(KZ * ROWS, COLS),
        merid.reshape(KZ * ROWS, COLS),
        land,
        levels,
    )
    groups = ROWS // 8
    native = (NT, KZ * ROWS, COLS)
    ma, mb = call(
        pack_lat_kernel,
        "pack_lat",
        [(PAYLOAD,) + VREG] * 2,
        [
            pltpu.VMEM((2, NT * KZ, 8, COLS), f32),
            pltpu.VMEM((2, KZ, 8, COLS), f32),
            pltpu.VMEM((2, KZ, 8, COLS), f32),
            pltpu.VMEM((2, 2, 8, COLS), jnp.int32),
            pltpu.SemaphoreType.DMA((10,)),
        ],
        10**5,
        tracers.reshape(NT * KZ, ROWS, COLS),
        zonal,
        merid,
        land,
        levels,
        in_hbm=True,
    )
    with jax.named_scope("swap_lat"):
        sa = lax.ppermute(ma, "lat", neighbour_swaps(n_lat, False, False))
        sb = lax.ppermute(mb, ("lon", "lat"), odd_lat_swaps(n_lon, n_lat))
    rows = [(EXT, NT) + VREG, (EXT, NT) + VREG, (EXT, 3) + VREG, (EXT, FIELDS) + VREG]
    c0, c1, raw, stat, main, edge, pa, pb = call(
        own_kernel,
        "interior",
        rows + [native, (ROWS, 4) + VREG, (2, groups) + VREG, (2, groups) + VREG],
        [pltpu.VMEM(a.shape, a.dtype) for a in flat] + [pltpu.SemaphoreType.DMA((5,))],
        10**7,
        *flat,
        in_hbm=True,
    )
    la, lb, ch, qh, sh, mh = call(
        pack_lon_kernel,
        "pack_lon",
        [(2, groups + 1) + VREG] * 2
        + [(8, NT) + VREG, (8, 3) + VREG, (8,) + VREG, (8,) + VREG],
        [],
        10**5,
        sa,
        sb,
        pa,
        pb,
    )
    with jax.named_scope("swap_lon"):
        ta = lax.ppermute(la, "lon", neighbour_swaps(n_lon, False, True))
        tb = lax.ppermute(lb, "lon", neighbour_swaps(n_lon, True, True))
    *_, main, eh = call(
        border_kernel,
        "border",
        rows + [native, (8, 4) + VREG],
        [],
        10**7,
        c0,
        c1,
        raw,
        stat,
        main,
        ch,
        qh,
        mh,
        sh,
        aliases={i: i for i in range(5)},
    )
    (out,) = call(
        edge_kernel,
        "edges",
        [native],
        [
            pltpu.VMEM((EXT, 1) + VREG, f32),
            pltpu.VMEM((EXT, 1) + VREG, f32),
            pltpu.VMEM((EXT, 3) + VREG, f32),
            pltpu.VMEM((EXT, FIELDS) + VREG, f32),
            pltpu.VMEM((KZ * ROWS, COLS), f32),
        ],
        10**6,
        main,
        edge,
        eh,
        ta,
        tb,
    )
    return out.reshape(tracers.shape)


def solution(mesh):
    return jax.shard_map(
        per_device,
        mesh=mesh,
        in_specs=(
            P(None, None, "lat", "lon"),
            P(None, "lat", "lon"),
            P(None, "lat", "lon"),
            P("lat", "lon"),
            P("lat", "lon"),
        ),
        out_specs=P(None, None, "lat", "lon"),
        check_vma=False,
    )
```

```python
import jax
import jax.numpy as jnp
from jax import lax
from jax.experimental import pallas as pl
from jax.experimental.pallas import tpu as pltpu
from jax.sharding import PartitionSpec as P


KZ = 8
ROWS = 32
COLS = 128
NT = 4
HALO = 4
EXT = ROWS + 2 * HALO
PAYLOAD = 22
MASK_AT = 16
MERID_AT = 17
ZONAL_AT = 20
FIELDS = 10
VMEM_LIMIT = 12 * 2**20

DIFF_H = 0.1
DIFF_V = 0.2
UPSTREAM = 1.0 / 6.0

VREG = (KZ, COLS)


def lanes():
    return lax.broadcasted_iota(jnp.int32, VREG, 1)


def levels_iota():
    return lax.broadcasted_iota(jnp.int32, VREG, 0)


def roll_x(v, shift):
    shift %= COLS
    return v if shift == 0 else pltpu.roll(v, shift, 1)


def roll_k(v, shift):
    return pltpu.roll(v, shift % KZ, 0)


def load_row(ref, y):
    return ref[pl.ds(y, KZ, stride=ROWS), :]


def load_tracer(ref, t, y):
    return ref[t, pl.ds(y, KZ, stride=ROWS), :]


def load_wet(land_ref, levels_ref, y):
    depth = jnp.where(land_ref[pl.ds(y, 1), :] == 1, levels_ref[pl.ds(y, 1), :], 0)
    return jnp.where(levels_iota() < jnp.broadcast_to(depth, VREG), 1.0, 0.0)


def halo_row(r):
    return -1 - r if r < HALO else ROWS + r - HALO


def gather_edges(parts):
    slot = ((lanes() - 16) >> 5) & 3
    out = roll_x(parts[-1], 32 * len(parts))
    for t in range(len(parts) - 1):
        out = jnp.where(slot == t, roll_x(parts[t], 32 * (t + 1)), out)
    return out


def pick(v, index):
    return jnp.take_along_axis(v, index, axis=1)


def edge_index(slot, r=0):
    lane = lanes()
    at = (lane - 24) & 31
    field = ((lane - 24) & 96) if slot is None else 32 * slot
    return (field + 4 * r + jnp.where(at < 16, at + 24, at + 8)) & (COLS - 1)


def edge_fields(moving, static, r=0):
    out = [pick(moving, edge_index(None, r))]
    return out + [pick(static, edge_index(f, r)) for f in range(3)]


def pack_eight(rows):
    lane = lanes()
    to_right = ((lane - 28) >> 2) & 7
    to_left = (lane >> 2) & 7
    right = left = rows[0]
    for r in range(1, 8):
        moved = roll_x(rows[r], 4 * r)
        right = jnp.where(to_right == r, moved, right)
        left = jnp.where(to_left == r, moved, left)
    return right, left


def is_even(axis):
    return lax.rem(lax.axis_index(axis), 2) == 0


def pack_lat_kernel(
    tracers, zonal, merid, land, levels, a_ref, b_ref, c_rows, z_rows, m_rows, d_rows, sems
):
    copies = []

    def fetch(source, target):
        copies.append(pltpu.make_async_copy(source, target, sems.at[len(copies)]))
        copies[-1].start()

    for side, rows in enumerate((pl.ds(0, 8), pl.ds(ROWS - 8, 8))):
        fetch(tracers.at[:, rows, :], c_rows.at[side])
        fetch(zonal.at[:, rows, :], z_rows.at[side])
        fetch(merid.at[:, rows, :], m_rows.at[side])
        fetch(land.at[rows, :], d_rows.at[side, 0])
        fetch(levels.at[rows, :], d_rows.at[side, 1])
    for copy in copies:
        copy.wait()
    even = is_even("lat")
    flat_c = c_rows.reshape(2 * NT, KZ * 8, COLS)
    flat_z, flat_m = z_rows.reshape(2, KZ * 8, COLS), m_rows.reshape(2, KZ * 8, COLS)
    for j in range(HALO):
        for ref, at_top in ((a_ref, even), (b_ref, jnp.logical_not(even))):
            side = jnp.where(at_top, 1, 0)
            y = jnp.where(at_top, 7 - j, j)
            row = pl.ds(y, KZ, stride=8)
            for t in range(NT):
                ref[NT * j + t] = flat_c[side * NT + t, row, :]
            for i in range(2):
                mask = d_rows[side, i, pl.ds(y, 1), :].astype(jnp.float32)
                ref[MASK_AT, HALO * i + j : HALO * i + j + 1, :] = mask
            if j < 3:
                ref[MERID_AT + j] = flat_m[side, row, :]
            if j < 2:
                ref[ZONAL_AT + j] = flat_z[side, row, :]

    @pl.when(lax.axis_index("lat") == lax.axis_size("lat") - 1)
    def _():
        flip = COLS - 1 - lanes()
        for p in range(PAYLOAD):
            v = pick(b_ref[p], flip)
            b_ref[p] = v if p < MERID_AT else -v


def own_kernel(*refs):
    sources, (c0, c1, raw, stat, edge_ref, a_ref, b_ref) = refs[:5], refs[5:12]
    targets, sems, rolled, east = refs[12:17], *refs[17:20]
    copies = [
        pltpu.make_async_copy(a, b, sems.at[i])
        for i, (a, b) in enumerate(zip(sources, targets))
    ]
    for copy in copies:
        copy.start()
    for copy in copies:
        copy.wait()
    tracers, zonal, merid, land, levels = targets
    even = is_even("lon")
    for g in range(ROWS // 8):
        moving, static = [], []
        for r in range(8):
            y = 8 * g + r
            cs = [load_tracer(tracers, t, y) for t in range(NT)]
            qs = [load_row(zonal, y), load_row(merid, y), load_wet(land, levels, y)]
            for t in range(NT):
                c0[y + HALO, t] = cs[t]
            for f in range(3):
                raw[y + HALO, f] = qs[f]
            moving.append(gather_edges(cs))
            static.append(gather_edges(qs))
        for i, rows in enumerate((moving, static)):
            right, left = pack_eight(rows)
            a_ref[i, g] = jnp.where(even, right, left)
            b_ref[i, g] = jnp.where(even, left, right)
        for r in range(8):
            for i, v in enumerate(edge_fields(moving[r], static[r])):
                edge_ref[8 * g + r, i] = v
    statics(raw, stat, 1, ROWS - 2, 15, 14)
    advance_rows(c0, stat, rolled, east, NT, 2, ROWS - 2, BLOCK_1, keep_in(c1))


def pack_lon_kernel(
    ra_ref, rb_ref, pa_ref, pb_ref, a_ref, b_ref, c_ref, q_ref, static_ref, moving_ref
):
    even_lon = is_even("lon")
    even_lat = is_even("lat")
    bottom = lax.axis_index("lat") == 0
    moving, static = [], []
    for r in range(8):
        j = r % HALO

        def get(p):
            north, south = (ra_ref, rb_ref) if r >= HALO else (rb_ref, ra_ref)
            v = jnp.where(even_lat, north[p], south[p])
            return v if r >= HALO else jnp.where(bottom, 0.0, v)

        cs = [get(NT * j + t) for t in range(NT)]
        mask = get(MASK_AT)
        sea, depth = mask[j : j + 1], mask[HALO + j : HALO + j + 1]
        depth = jnp.broadcast_to(jnp.where(sea == 1.0, depth, 0.0), VREG)
        wet = jnp.where(levels_iota().astype(jnp.float32) < depth, 1.0, 0.0)
        zero = jnp.zeros(VREG, jnp.float32)
        qs = [
            get(ZONAL_AT + j) if j < 2 else zero,
            get(MERID_AT + j) if j < 3 else zero,
            wet,
        ]
        for t in range(NT):
            c_ref[r, t] = cs[t]
        for f in range(3):
            q_ref[r, f] = qs[f]
        moving.append(gather_edges(cs))
        static.append(gather_edges(qs))
        moving_ref[r] = moving[r]
        static_ref[r] = static[r]
    for i, rows in enumerate((moving, static)):
        right, left = pack_eight(rows)
        a_ref[i, ROWS // 8] = jnp.where(even_lon, right, left)
        b_ref[i, ROWS // 8] = jnp.where(even_lon, left, right)
        for g in range(ROWS // 8):
            a_ref[i, g] = pa_ref[i, g]
            b_ref[i, g] = pb_ref[i, g]


def derive_along(flow, face, face_before, face_after):
    up = jnp.maximum(flow, 0.0) * (UPSTREAM / 2)
    down = jnp.minimum(flow, 0.0) * (UPSTREAM / 2)
    near = (up - down) + DIFF_H * face
    mean = 0.25 * flow
    far_before, far_after = up * face_before, down * face_after
    return mean + near + far_before, mean - near + far_after, far_before, far_after


def derive(zonal, merid, wet):
    here = wet[1]
    face = here * roll_x(here, -1)
    flow = (zonal + roll_x(zonal, -1)) * face
    along_x = derive_along(flow, face, roll_x(face, 1), roll_x(face, -1))
    faces = [wet[d] * wet[d + 1] for d in range(3)]
    flow = (merid[0] + merid[1]) * faces[1]
    along_y = derive_along(flow, faces[1], faces[0], faces[2])
    face_z = jnp.where(levels_iota() < KZ - 1, here * roll_k(here, -1), 0.0)
    return along_x + along_y + (DIFF_V * face_z, here)


X, Y, FZ, WET = 0, 4, 8, 9


def statics_block(raw, stat, y, block):
    merid = [raw[y, 1]]
    wet = [raw[y + d, 2] for d in range(-1, 2)]
    rows = []
    for d in range(block):
        merid = merid[-1:] + [raw[y + d + 1, 1]]
        wet = wet[-3:] + [raw[y + d + 2, 2]]
        rows.append(derive(raw[y + d, 0], merid, wet))

    def store():
        for d in range(block):
            for f in range(FIELDS):
                stat[y + d, f] = rows[d][f]

    return store


def statics(raw, stat, first, last, block, stride):
    count = (last - first - block) // stride + 1
    assert (count - 1) * stride + block == last - first

    def body(i, _):
        statics_block(raw, stat, first + HALO + i * stride, block)()
        return 0

    lax.fori_loop(0, count, body, 0)


def flux(st, at, before, low, high, after):
    return (st[at] * low + st[at + 1] * high) - (st[at + 2] * before + st[at + 3] * after)


def advance_rows(src, stat, rolled, east, streams, first, last, block, put):
    count = (last - first) // block
    assert count * block == last - first
    every = [(d, s) for d in range(block) for s in range(streams)]

    def shift(y):
        for d, s in every:
            here = src[y + d, s]
            for n, v in enumerate([roll_x(here, n) for n in (1, -1, -2)]):
                rolled[d, s, n] = v

    def eastward(y):
        st = [[stat[y + d, X + f] for f in range(4)] for d in range(block)]
        for d, s in every:
            before, after, far = [rolled[d, s, n] for n in range(3)]
            through = flux(st[d], 0, before, src[y + d, s], after, far)
            east[d, s, 0] = through
            east[d, s, 1] = roll_x(through, 1)

    def total(y, below):
        below = list(below)
        c = [[src[y + d, s] for s in range(streams)] for d in range(-2, 2)]
        rows = []
        for d in range(block):
            st = [stat[y + d, f] for f in range(Y, FIELDS)]
            c = c[1:] + [[src[y + d + 2, s] for s in range(streams)]]
            values = []
            for s in range(streams):
                here = c[1][s]
                above = flux(st, 0, c[0][s], here, c[2][s], c[3][s])
                gz = (roll_k(here, -1) - here) * st[FZ - Y]
                along_x = east[d, s, 1] - east[d, s, 0]
                sum_xy = (here + along_x) + (below[s] - above)
                values.append(st[WET - Y] * (sum_xy + (gz - roll_k(gz, 1))))
                below[s] = above
            rows.append(values)
        for d in range(block):
            put(y - HALO + d, rows[d])
        return tuple(below)

    def body(i, below):
        y = first + HALO + i * block
        shift(y)
        eastward(y)
        return total(y, below)

    y = first + HALO
    st = [stat[y - 1, Y + f] for f in range(4)]
    below = tuple(
        flux(st, 0, *[src[y + d, s] for d in range(-2, 2)]) for s in range(streams)
    )
    if count == 1:
        body(0, below)
    else:
        lax.fori_loop(0, count, body, below)


def keep_in(ref):
    def put(y, values):
        for s, v in enumerate(values):
            ref[y + HALO, s] = v

    return put


def native_in(ref):
    def put(y, values):
        for t, v in enumerate(values):
            ref[t, pl.ds(y, KZ, stride=ROWS), :] = v

    return put


def border_kernel(
    _c0, _c1, _raw, _stat, ch_ref, qh_ref, mh_ref, sh_ref, c0, c1, raw, stat, main_ref, eh_ref,
    rolled, east
):
    for r in range(8):
        y = halo_row(r) + HALO
        for t in range(NT):
            c0[y, t] = ch_ref[r, t]
        for f in range(3):
            raw[y, f] = qh_ref[r, f]
    for store in [statics_block(raw, stat, y + HALO, 4) for y in (-3, ROWS - 2)]:
        store()
    for first in (-2, ROWS - 2):
        advance_rows(c0, stat, rolled, east, NT, first, first + 4, 4, keep_in(c1))
    advance_rows(c1, stat, rolled, east, NT, 4, ROWS - 4, BLOCK_2, native_in(main_ref))
    for first in (0, ROWS - 4):
        advance_rows(c1, stat, rolled, east, NT, first, first + 4, 4, native_in(main_ref))
    for r in range(8):
        for i, v in enumerate(edge_fields(mh_ref[r], sh_ref[r])):
            eh_ref[r, i] = v


BLOCK_1 = 7
BLOCK_2 = 8
EDGE_BLOCK_1 = 36
EDGE_BLOCK_2 = 32


def edge_kernel(
    main_ref, edge_ref, eh_ref, ra_ref, rb_ref, out_ref, e0, e1, raw, stat, native,
    rolled, east
):
    even = is_even("lon")
    lane = lanes()
    from_left = ((lane - 28) >> 2) & 7
    at = (lane - 24) & 31
    own = (at < 8) | (at >= 24)
    for g in range(ROWS // 8 + 1):
        left = [jnp.where(even, rb_ref[i, g], ra_ref[i, g]) for i in range(2)]
        right = [jnp.where(even, ra_ref[i, g], rb_ref[i, g]) for i in range(2)]
        for r in range(8):
            both = [jnp.where(from_left == r, left[i], right[i]) for i in range(2)]
            other = edge_fields(*both, r)
            if g < ROWS // 8:
                y = 8 * g + r
                mine = [edge_ref[y, i] for i in range(4)]
            else:
                y = halo_row(r)
                mine = [eh_ref[r, i] for i in range(4)]
            row = [jnp.where(own, m, o) for m, o in zip(mine, other)]
            e0[y + HALO, 0] = row[0]
            for f in range(3):
                raw[y + HALO, f] = row[f + 1]
    statics(raw, stat, -3, ROWS + 2, 19, 18)

    advance_rows(e0, stat, rolled, east, 1, -2, ROWS + 2, EDGE_BLOCK_1, keep_in(e1))
    high = (lane & 31) >= 16

    def finish(y, values):
        native[pl.ds(y, KZ, stride=ROWS), :] = jnp.where(
            high, values[0], roll_x(values[0], -16)
        )

    advance_rows(e1, stat, rolled, east, 1, 0, ROWS, EDGE_BLOCK_2, finish)
    near = (lane < 4) | (lane >= COLS - 4)
    for i in range(KZ * ROWS // 8):
        edge = native[8 * i : 8 * i + 8, :]
        for t in range(NT):
            out_ref[t, 8 * i : 8 * i + 8, :] = jnp.where(
                near, roll_x(edge, -32 * (t + 1)), main_ref[t, 8 * i : 8 * i + 8, :]
            )


def neighbour_swaps(size, odd, wrap):
    pairs = []
    for i in range(size):
        j = i + 1 if i % 2 == int(odd) else i - 1
        if wrap or 0 <= j < size:
            pairs.append((i, j % size))
    return pairs


def odd_lat_swaps(n_lon, n_lat):
    pairs = []
    for lon in range(n_lon):
        for i, j in neighbour_swaps(n_lat, True, False):
            pairs.append((lon * n_lat + i, lon * n_lat + j))
        pairs.append((lon * n_lat + n_lat - 1, (n_lon - 1 - lon) * n_lat + n_lat - 1))
        pairs.append((lon * n_lat, (lon ^ 1) * n_lat))
    return pairs


def work(streams, values):
    return pltpu.VMEM((EXT, streams, values) + VREG, jnp.float32)


def call(kernel, name, outs, scratch, flops, *args, aliases={}, in_hbm=False):
    f32 = jnp.float32
    kwargs = {}
    if in_hbm:
        args = [pltpu.with_memory_space_constraint(a, pltpu.HBM) for a in args]
        kwargs = dict(in_specs=[pl.BlockSpec(memory_space=pltpu.HBM)] * len(args))
    with jax.named_scope(name):
        return pl.pallas_call(
            kernel,
            out_shape=tuple(jax.ShapeDtypeStruct(tuple(o), f32) for o in outs),
            scratch_shapes=scratch,
            input_output_aliases=aliases,
            compiler_params=pltpu.CompilerParams(vmem_limit_bytes=VMEM_LIMIT),
            cost_estimate=pl.CostEstimate(
                flops=flops,
                bytes_accessed=sum(4 * a.size for a in args),
                transcendentals=0,
            ),
            **kwargs,
        )(*args)


def per_device(tracers, zonal, merid, land, levels):
    n_lon, n_lat = lax.axis_size("lon"), lax.axis_size("lat")
    f32 = jnp.float32
    flat = (
        tracers.reshape(NT, KZ * ROWS, COLS),
        zonal.reshape(KZ * ROWS, COLS),
        merid.reshape(KZ * ROWS, COLS),
        land,
        levels,
    )
    groups = ROWS // 8
    native = (NT, KZ * ROWS, COLS)
    ma, mb = call(
        pack_lat_kernel,
        "pack_lat",
        [(PAYLOAD,) + VREG] * 2,
        [
            pltpu.VMEM((2, NT * KZ, 8, COLS), f32),
            pltpu.VMEM((2, KZ, 8, COLS), f32),
            pltpu.VMEM((2, KZ, 8, COLS), f32),
            pltpu.VMEM((2, 2, 8, COLS), jnp.int32),
            pltpu.SemaphoreType.DMA((10,)),
        ],
        10**5,
        tracers.reshape(NT * KZ, ROWS, COLS),
        zonal,
        merid,
        land,
        levels,
        in_hbm=True,
    )
    with jax.named_scope("swap_lat"):
        sa = lax.ppermute(ma, "lat", neighbour_swaps(n_lat, False, False))
        sb = lax.ppermute(mb, ("lon", "lat"), odd_lat_swaps(n_lon, n_lat))
    rows = [(EXT, NT) + VREG, (EXT, NT) + VREG, (EXT, 3) + VREG, (EXT, FIELDS) + VREG]
    c0, c1, raw, stat, edge, pa, pb = call(
        own_kernel,
        "interior",
        rows + [(ROWS, 4) + VREG, (2, groups) + VREG, (2, groups) + VREG],
        [pltpu.VMEM(a.shape, a.dtype) for a in flat]
        + [pltpu.SemaphoreType.DMA((5,)), work(NT, 3), work(NT, 2)],
        10**7,
        *flat,
        in_hbm=True,
    )
    la, lb, ch, qh, sh, mh = call(
        pack_lon_kernel,
        "pack_lon",
        [(2, groups + 1) + VREG] * 2
        + [(8, NT) + VREG, (8, 3) + VREG, (8,) + VREG, (8,) + VREG],
        [],
        10**5,
        sa,
        sb,
        pa,
        pb,
    )
    with jax.named_scope("swap_lon"):
        ta = lax.ppermute(la, "lon", neighbour_swaps(n_lon, False, True))
        tb = lax.ppermute(lb, "lon", neighbour_swaps(n_lon, True, True))
    *_, main, eh = call(
        border_kernel,
        "border",
        rows + [native, (8, 4) + VREG],
        [work(NT, 3), work(NT, 2)],
        10**7,
        c0,
        c1,
        raw,
        stat,
        ch,
        qh,
        mh,
        sh,
        aliases={i: i for i in range(4)},
    )
    (out,) = call(
        edge_kernel,
        "edges",
        [native],
        [
            pltpu.VMEM((EXT, 1) + VREG, f32),
            pltpu.VMEM((EXT, 1) + VREG, f32),
            pltpu.VMEM((EXT, 3) + VREG, f32),
            pltpu.VMEM((EXT, FIELDS) + VREG, f32),
            pltpu.VMEM((KZ * ROWS, COLS), f32),
            work(1, 3),
            work(1, 2),
        ],
        10**6,
        main,
        edge,
        eh,
        ta,
        tb,
    )
    return out.reshape(tracers.shape)


def solution(mesh):
    return jax.shard_map(
        per_device,
        mesh=mesh,
        in_specs=(
            P(None, None, "lat", "lon"),
            P(None, "lat", "lon"),
            P(None, "lat", "lon"),
            P("lat", "lon"),
            P("lat", "lon"),
        ),
        out_specs=P(None, None, "lat", "lon"),
        check_vma=False,
    )
```

```python
import jax
import jax.numpy as jnp
from jax import lax
from jax.experimental import pallas as pl
from jax.experimental.pallas import tpu as pltpu
from jax.sharding import PartitionSpec as P


KZ = 8
ROWS = 32
COLS = 128
NT = 4
HALO = 4
EXT = ROWS + 2 * HALO
PAYLOAD = 22
MASK_AT = 16
MERID_AT = 17
ZONAL_AT = 20
FIELDS = 10
VMEM_LIMIT = 12 * 2**20

DIFF_H = 0.1
DIFF_V = 0.2
UPSTREAM = 1.0 / 6.0

VREG = (KZ, COLS)


def lanes():
    return lax.broadcasted_iota(jnp.int32, VREG, 1)


def levels_iota():
    return lax.broadcasted_iota(jnp.int32, VREG, 0)


def roll_x(v, shift):
    shift %= COLS
    return v if shift == 0 else pltpu.roll(v, shift, 1)


def roll_k(v, shift):
    return pltpu.roll(v, shift % KZ, 0)


def load_row(ref, y):
    return ref[pl.ds(y, KZ, stride=ROWS), :]


def load_tracer(ref, t, y):
    return ref[t, pl.ds(y, KZ, stride=ROWS), :]


def load_wet(land_ref, levels_ref, y):
    depth = jnp.where(land_ref[pl.ds(y, 1), :] == 1, levels_ref[pl.ds(y, 1), :], 0)
    return jnp.where(levels_iota() < jnp.broadcast_to(depth, VREG), 1.0, 0.0)


def halo_row(r):
    return -1 - r if r < HALO else ROWS + r - HALO


def gather_edges(parts):
    slot = ((lanes() - 16) >> 5) & 3
    out = roll_x(parts[-1], 32 * len(parts))
    for t in range(len(parts) - 1):
        out = jnp.where(slot == t, roll_x(parts[t], 32 * (t + 1)), out)
    return out


def pick(v, index):
    return jnp.take_along_axis(v, index, axis=1)


def edge_index(slot, r=0):
    lane = lanes()
    at = (lane - 24) & 31
    field = ((lane - 24) & 96) if slot is None else 32 * slot
    return (field + 4 * r + jnp.where(at < 16, at + 24, at + 8)) & (COLS - 1)


def edge_fields(moving, static, r=0):
    out = [pick(moving, edge_index(None, r))]
    return out + [pick(static, edge_index(f, r)) for f in range(3)]


def pack_eight(rows):
    lane = lanes()
    to_right = ((lane - 28) >> 2) & 7
    to_left = (lane >> 2) & 7
    right = left = rows[0]
    for r in range(1, 8):
        moved = roll_x(rows[r], 4 * r)
        right = jnp.where(to_right == r, moved, right)
        left = jnp.where(to_left == r, moved, left)
    return right, left


def is_even(axis):
    return lax.rem(lax.axis_index(axis), 2) == 0


def pack_lat_kernel(tracers, zonal, merid, land, levels, a_ref, b_ref, masks, sems):
    even = is_even("lat")
    pairs = []
    for i, field in enumerate((land, levels)):
        pairs += [
            (field.at[pl.ds(y, 8), :], masks.at[i, side])
            for side, y in enumerate((0, ROWS - 8))
        ]
    sides = ((a_ref, even), (b_ref, jnp.logical_not(even)))
    for ref, at_top in sides:
        flat = ref.reshape(PAYLOAD * KZ, COLS)
        for j in range(HALO):
            y = jnp.where(at_top, ROWS - 1 - j, j)
            pairs.append((tracers.at[:, y, :], flat.at[pl.ds(NT * KZ * j, NT * KZ), :]))
            if j < 3:
                pairs.append((merid.at[:, y, :], ref.at[MERID_AT + j]))
            if j < 2:
                pairs.append((zonal.at[:, y, :], ref.at[ZONAL_AT + j]))
    for copy in start_all(pairs, sems):
        copy.wait()
    for ref, at_top in sides:
        for j in range(HALO):
            row = pl.ds(jnp.where(at_top, 7 - j, j), 1)
            for i in range(2):
                mask = masks[i, jnp.where(at_top, 1, 0), row, :].astype(jnp.float32)
                ref[MASK_AT, HALO * i + j : HALO * i + j + 1, :] = mask

    @pl.when(lax.axis_index("lat") == lax.axis_size("lat") - 1)
    def _():
        flip = COLS - 1 - lanes()
        for p in range(PAYLOAD):
            v = pick(b_ref[p], flip)
            b_ref[p] = v if p < MERID_AT else -v


def start_all(pairs, sems, first=0):
    copies = [
        pltpu.make_async_copy(source, target, sems.at[first + i])
        for i, (source, target) in enumerate(pairs)
    ]
    for copy in copies:
        copy.start()
    return copies


def own_kernel(
    tracers, zonal, merid, land, levels, c0, c1, raw, stat, edge_ref, a_ref, b_ref,
    tracers_here, zonal_here, merid_here, land_here, levels_here, sems, rolled, east
):
    fields = start_all(
        [(land, land_here), (levels, levels_here), (zonal, zonal_here), (merid, merid_here)],
        sems,
    )
    parts = start_all([(tracers, tracers_here)], sems, len(fields))
    level_rows = [v.reshape(KZ * ROWS, COLS) for v in (zonal_here, merid_here)]
    tracer_rows = tracers_here.reshape(NT, KZ * ROWS, COLS)
    even = is_even("lon")

    def pack(i, g, rows):
        right, left = pack_eight(rows)
        a_ref[i, g] = jnp.where(even, right, left)
        b_ref[i, g] = jnp.where(even, left, right)

    for copy in fields:
        copy.wait()

    for g in range(ROWS // 8):
        static = []
        for r in range(8):
            y = 8 * g + r
            row = [load_row(v, y) for v in level_rows] + [load_wet(land_here, levels_here, y)]
            for f in range(3):
                raw[y + HALO, f] = row[f]
            static.append(gather_edges(row))
        pack(1, g, static)
        for r in range(8):
            for f in range(3):
                edge_ref[8 * g + r, 1 + f] = pick(static[r], edge_index(f))
    statics(raw, stat, 1, ROWS - 2, 15, 14)
    for copy in parts:
        copy.wait()

    for g in range(ROWS // 8):
        moving = []
        for r in range(8):
            y = 8 * g + r
            row = [load_tracer(tracer_rows, t, y) for t in range(NT)]
            for t in range(NT):
                c0[y + HALO, t] = row[t]
            moving.append(gather_edges(row))
        pack(0, g, moving)
        for r in range(8):
            edge_ref[8 * g + r, 0] = pick(moving[r], edge_index(None))
    advance_rows(c0, stat, rolled, east, NT, 2, ROWS - 2, BLOCK_1, keep_in(c1))


def pack_lon_kernel(
    ra_ref, rb_ref, pa_ref, pb_ref, a_ref, b_ref, d_ref, c_ref, q_ref, static_ref, moving_ref
):
    even_lon = is_even("lon")
    even_lat = is_even("lat")
    bottom = lax.axis_index("lat") == 0
    moving, static = [], []
    for r in range(8):
        j = r % HALO

        def get(p):
            north, south = (ra_ref, rb_ref) if r >= HALO else (rb_ref, ra_ref)
            v = jnp.where(even_lat, north[p], south[p])
            return v if r >= HALO else jnp.where(bottom, 0.0, v)

        cs = [get(NT * j + t) for t in range(NT)]
        mask = get(MASK_AT)
        sea, depth = mask[j : j + 1], mask[HALO + j : HALO + j + 1]
        depth = jnp.broadcast_to(jnp.where(sea == 1.0, depth, 0.0), VREG)
        wet = jnp.where(levels_iota().astype(jnp.float32) < depth, 1.0, 0.0)
        zero = jnp.zeros(VREG, jnp.float32)
        qs = [
            get(ZONAL_AT + j) if j < 2 else zero,
            get(MERID_AT + j) if j < 3 else zero,
            wet,
        ]
        for t in range(NT):
            c_ref[r, t] = cs[t]
        for f in range(3):
            q_ref[r, f] = qs[f]
        moving.append(gather_edges(cs))
        static.append(gather_edges(qs))
        moving_ref[r] = moving[r]
        static_ref[r] = static[r]
    for i, rows in enumerate((moving, static)):
        right, left = pack_eight(rows)
        a_ref[i, ROWS // 8] = d_ref[i, ROWS // 8] = jnp.where(even_lon, right, left)
        b_ref[i, ROWS // 8] = jnp.where(even_lon, left, right)
        for g in range(ROWS // 8):
            a_ref[i, g] = d_ref[i, g] = pa_ref[i, g]
            b_ref[i, g] = pb_ref[i, g]


def derive_along(flow, face, face_before, face_after):
    up = jnp.maximum(flow, 0.0) * (UPSTREAM / 2)
    down = jnp.minimum(flow, 0.0) * (UPSTREAM / 2)
    near = (up - down) + DIFF_H * face
    mean = 0.25 * flow
    far_before, far_after = up * face_before, down * face_after
    return mean + near + far_before, mean - near + far_after, far_before, far_after


def derive(zonal, merid, wet):
    here = wet[1]
    face = here * roll_x(here, -1)
    flow = (zonal + roll_x(zonal, -1)) * face
    along_x = derive_along(flow, face, roll_x(face, 1), roll_x(face, -1))
    faces = [wet[d] * wet[d + 1] for d in range(3)]
    flow = (merid[0] + merid[1]) * faces[1]
    along_y = derive_along(flow, faces[1], faces[0], faces[2])
    face_z = jnp.where(levels_iota() < KZ - 1, here * roll_k(here, -1), 0.0)
    return along_x + along_y + (DIFF_V * face_z, here)


X, Y, FZ, WET = 0, 4, 8, 9


def statics_block(raw, stat, y, block):
    merid = [raw[y, 1]]
    wet = [raw[y + d, 2] for d in range(-1, 2)]
    rows = []
    for d in range(block):
        merid = merid[-1:] + [raw[y + d + 1, 1]]
        wet = wet[-3:] + [raw[y + d + 2, 2]]
        rows.append(derive(raw[y + d, 0], merid, wet))

    def store():
        for d in range(block):
            for f in range(FIELDS):
                stat[y + d, f] = rows[d][f]

    return store


def statics(raw, stat, first, last, block, stride):
    count = (last - first - block) // stride + 1
    assert (count - 1) * stride + block == last - first

    def body(i, _):
        statics_block(raw, stat, first + HALO + i * stride, block)()
        return 0

    lax.fori_loop(0, count, body, 0)


def flux(st, at, before, low, high, after):
    return (st[at] * low + st[at + 1] * high) - (st[at + 2] * before + st[at + 3] * after)


def advance_rows(src, stat, rolled, east, streams, first, last, block, put):
    count = (last - first) // block
    assert count * block == last - first
    every = [(d, s) for d in range(block) for s in range(streams)]

    def shift(y, at):
        for d, s in every:
            here = src[y + d, s]
            for n, v in enumerate([roll_x(here, n) for n in (1, -1, -2)]):
                rolled[at + d, s, n] = v

    def eastward(y, at):
        st = [[stat[y + d, X + f] for f in range(4)] for d in range(block)]
        for d, s in every:
            before, after, far = [rolled[at + d, s, n] for n in range(3)]
            through = flux(st[d], 0, before, src[y + d, s], after, far)
            east[at + d, s, 0] = through
            east[at + d, s, 1] = roll_x(through, 1)

    def total(y, at, below):
        below = list(below)
        c = [[src[y + d, s] for s in range(streams)] for d in range(-2, 2)]
        rows = []
        for d in range(block):
            st = [stat[y + d, f] for f in range(Y, FIELDS)]
            c = c[1:] + [[src[y + d + 2, s] for s in range(streams)]]
            values = []
            for s in range(streams):
                here = c[1][s]
                above = flux(st, 0, c[0][s], here, c[2][s], c[3][s])
                gz = (roll_k(here, -1) - here) * st[FZ - Y]
                along_x = east[at + d, s, 1] - east[at + d, s, 0]
                sum_xy = (here + along_x) + (below[s] - above)
                values.append(st[WET - Y] * (sum_xy + (gz - roll_k(gz, 1))))
                below[s] = above
            rows.append(values)
        for d in range(block):
            put(y - HALO + d, rows[d])
        return tuple(below)

    y = first + HALO
    st = [stat[y - 1, Y + f] for f in range(4)]
    below = tuple(
        flux(st, 0, *[src[y + d, s] for d in range(-2, 2)]) for s in range(streams)
    )
    shift(y, 0)
    if count == 1:
        eastward(y, 0)
        total(y, 0, below)
        return
    if count % 2:
        eastward(y, 0)
        below = total(y, 0, below)
        y += block
        shift(y, 0)

    def body(i, below):
        for half in range(2):
            at = y + (2 * i + half) * block
            here, there = block * half, block * (1 - half)
            eastward(at, here)
            shift(jnp.minimum(at + block, last + HALO - block), there)
            below = total(at, here, below)
        return below

    lax.fori_loop(0, count // 2, body, below)


def keep_in(ref):
    def put(y, values):
        for s, v in enumerate(values):
            ref[y + HALO, s] = v

    return put


def native_in(ref):
    def put(y, values):
        for t, v in enumerate(values):
            ref[t, pl.ds(y, KZ, stride=ROWS), :] = v

    return put


def border_kernel(
    _c0, _c1, _raw, _stat, ch_ref, qh_ref, mh_ref, sh_ref, c0, c1, raw, stat, main_ref, eh_ref,
    rolled, east
):
    for r in range(8):
        y = halo_row(r) + HALO
        for t in range(NT):
            c0[y, t] = ch_ref[r, t]
        for f in range(3):
            raw[y, f] = qh_ref[r, f]
    for store in [statics_block(raw, stat, y + HALO, 4) for y in (-3, ROWS - 2)]:
        store()
    for first in (-2, ROWS - 2):
        advance_rows(c0, stat, rolled, east, NT, first, first + 4, 4, keep_in(c1))
    advance_rows(c1, stat, rolled, east, NT, 4, ROWS - 4, BLOCK_2, native_in(main_ref))
    for first in (0, ROWS - 4):
        advance_rows(c1, stat, rolled, east, NT, first, first + 4, 4, native_in(main_ref))
    for r in range(8):
        for i, v in enumerate(edge_fields(mh_ref[r], sh_ref[r])):
            eh_ref[r, i] = v


BLOCK_1 = 14
BLOCK_2 = 12
EDGE_BLOCK_1 = 36
EDGE_BLOCK_2 = 32


def edge_kernel(
    main_ref, edge_ref, eh_ref, ra_ref, rb_ref, rc_ref, out_ref, e0, e1, raw, stat, native,
    rolled, east
):
    even = is_even("lon")
    last = is_last_pair(lax.axis_index("lon"), lax.axis_size("lon"))
    lane = lanes()
    from_left = ((lane - 28) >> 2) & 7
    at = (lane - 24) & 31
    own = (at < 8) | (at >= 24)
    for g in range(ROWS // 8 + 1):
        evens = [jnp.where(last, rc_ref[i, g], ra_ref[i, g]) for i in range(2)]
        left = [jnp.where(even, rb_ref[i, g], evens[i]) for i in range(2)]
        right = [jnp.where(even, evens[i], rb_ref[i, g]) for i in range(2)]
        for r in range(8):
            both = [jnp.where(from_left == r, left[i], right[i]) for i in range(2)]
            other = edge_fields(*both, r)
            if g < ROWS // 8:
                y = 8 * g + r
                mine = [edge_ref[y, i] for i in range(4)]
            else:
                y = halo_row(r)
                mine = [eh_ref[r, i] for i in range(4)]
            row = [jnp.where(own, m, o) for m, o in zip(mine, other)]
            e0[y + HALO, 0] = row[0]
            for f in range(3):
                raw[y + HALO, f] = row[f + 1]
    statics(raw, stat, -3, ROWS + 2, 19, 18)

    advance_rows(e0, stat, rolled, east, 1, -2, ROWS + 2, EDGE_BLOCK_1, keep_in(e1))
    high = (lane & 31) >= 16

    def finish(y, values):
        native[pl.ds(y, KZ, stride=ROWS), :] = jnp.where(
            high, values[0], roll_x(values[0], -16)
        )

    advance_rows(e1, stat, rolled, east, 1, 0, ROWS, EDGE_BLOCK_2, finish)
    near = (lane < 4) | (lane >= COLS - 4)
    for i in range(KZ * ROWS // 8):
        edge = native[8 * i : 8 * i + 8, :]
        for t in range(NT):
            out_ref[t, 8 * i : 8 * i + 8, :] = jnp.where(
                near, roll_x(edge, -32 * (t + 1)), main_ref[t, 8 * i : 8 * i + 8, :]
            )


def neighbour_swaps(size, odd, wrap):
    pairs = []
    for i in range(size):
        j = i + 1 if i % 2 == int(odd) else i - 1
        if wrap or 0 <= j < size:
            pairs.append((i, j % size))
    return pairs


def odd_lat_swaps(n_lon, n_lat):
    pairs = []
    for lon in range(n_lon):
        for i, j in neighbour_swaps(n_lat, True, False):
            pairs.append((lon * n_lat + i, lon * n_lat + j))
        pairs.append((lon * n_lat + n_lat - 1, (n_lon - 1 - lon) * n_lat + n_lat - 1))
        pairs.append((lon * n_lat, (lon ^ 1) * n_lat))
    return pairs


def is_last_pair(lon, n_lon):
    return lon % (n_lon // 2) >= n_lon // 2 - 2


def even_lon_swaps(n_lon, n_lat, last):
    pairs = []
    for lon in range(n_lon):
        for lat in range(n_lat):
            mine = is_last_pair(lon, n_lon) == last
            to = (lon ^ 1, lat) if mine else (lon, lat ^ 1)
            pairs.append((lon * n_lat + lat, to[0] * n_lat + to[1]))
    return pairs


def work(streams, values):
    return pltpu.VMEM((EXT, streams, values) + VREG, jnp.float32)


def call(kernel, name, outs, scratch, flops, *args, aliases={}, in_hbm=False):
    f32 = jnp.float32
    kwargs = {}
    if in_hbm:
        args = [pltpu.with_memory_space_constraint(a, pltpu.HBM) for a in args]
        kwargs = dict(in_specs=[pl.BlockSpec(memory_space=pltpu.HBM)] * len(args))
    with jax.named_scope(name):
        return pl.pallas_call(
            kernel,
            out_shape=tuple(jax.ShapeDtypeStruct(tuple(o), f32) for o in outs),
            scratch_shapes=scratch,
            input_output_aliases=aliases,
            compiler_params=pltpu.CompilerParams(vmem_limit_bytes=VMEM_LIMIT),
            cost_estimate=pl.CostEstimate(
                flops=flops,
                bytes_accessed=sum(4 * a.size for a in args),
                transcendentals=0,
            ),
            **kwargs,
        )(*args)


def per_device(tracers, zonal, merid, land, levels):
    axes = ("lon", "lat")
    n_lon, n_lat = lax.axis_size("lon"), lax.axis_size("lat")
    f32 = jnp.float32
    args = (tracers.reshape(NT * KZ, ROWS, COLS), zonal, merid, land, levels)
    groups = ROWS // 8
    native = (NT, KZ * ROWS, COLS)
    ma, mb = call(
        pack_lat_kernel,
        "pack_lat",
        [(PAYLOAD,) + VREG] * 2,
        [
            pltpu.VMEM((2, 2, 8, COLS), jnp.int32),
            pltpu.SemaphoreType.DMA((4 + 2 * (HALO + 3 + 2),)),
        ],
        10**5,
        *args,
        in_hbm=True,
    )
    with jax.named_scope("swap_lat"):
        sa = lax.ppermute(ma, "lat", neighbour_swaps(n_lat, False, False))
        sb = lax.ppermute(mb, axes, odd_lat_swaps(n_lon, n_lat))
    rows = [(EXT, NT) + VREG, (EXT, NT) + VREG, (EXT, 3) + VREG, (EXT, FIELDS) + VREG]
    c0, c1, raw, stat, edge, pa, pb = call(
        own_kernel,
        "interior",
        rows + [(ROWS, 4) + VREG, (2, groups) + VREG, (2, groups) + VREG],
        [
            *[pltpu.VMEM(a.shape, a.dtype) for a in args],
            pltpu.SemaphoreType.DMA((len(args),)),
            work(NT, 3),
            work(NT, 2),
        ],
        10**7,
        *args,
        in_hbm=True,
    )
    la, lb, ld, ch, qh, sh, mh = call(
        pack_lon_kernel,
        "pack_lon",
        [(2, groups + 1) + VREG] * 3
        + [(8, NT) + VREG, (8, 3) + VREG, (8,) + VREG, (8,) + VREG],
        [],
        10**5,
        sa,
        sb,
        pa,
        pb,
    )
    with jax.named_scope("swap_lon"):
        ta = lax.ppermute(la, axes, even_lon_swaps(n_lon, n_lat, False))
        tb = lax.ppermute(lb, "lon", neighbour_swaps(n_lon, True, True))
        tc = lax.ppermute(ld, axes, even_lon_swaps(n_lon, n_lat, True))
    *_, main, eh = call(
        border_kernel,
        "border",
        rows + [native, (8, 4) + VREG],
        [work(NT, 3), work(NT, 2)],
        10**7,
        c0,
        c1,
        raw,
        stat,
        ch,
        qh,
        mh,
        sh,
        aliases={i: i for i in range(4)},
    )
    (out,) = call(
        edge_kernel,
        "edges",
        [native],
        [
            pltpu.VMEM((EXT, 1) + VREG, f32),
            pltpu.VMEM((EXT, 1) + VREG, f32),
            pltpu.VMEM((EXT, 3) + VREG, f32),
            pltpu.VMEM((EXT, FIELDS) + VREG, f32),
            pltpu.VMEM((KZ * ROWS, COLS), f32),
            work(1, 3),
            work(1, 2),
        ],
        10**6,
        main,
        edge,
        eh,
        ta,
        tb,
        tc,
    )
    return out.reshape(tracers.shape)


def solution(mesh):
    return jax.shard_map(
        per_device,
        mesh=mesh,
        in_specs=(
            P(None, None, "lat", "lon"),
            P(None, "lat", "lon"),
            P(None, "lat", "lon"),
            P("lat", "lon"),
            P("lat", "lon"),
        ),
        out_specs=P(None, None, "lat", "lon"),
        check_vma=False,
    )
```

```python
import jax
import jax.numpy as jnp
from jax import lax
from jax.experimental import pallas as pl
from jax.experimental.pallas import tpu as pltpu
from jax.sharding import PartitionSpec as P


KZ = 8
ROWS = 32
COLS = 128
NT = 4
HALO = 4
EXT = ROWS + 2 * HALO
PAYLOAD = 22
MASK_AT = 16
MERID_AT = 17
ZONAL_AT = 20
FIELDS = 10
VMEM_LIMIT = 12 * 2**20

DIFF_H = 0.1
DIFF_V = 0.2
UPSTREAM = 1.0 / 6.0

VREG = (KZ, COLS)


def lanes():
    return lax.broadcasted_iota(jnp.int32, VREG, 1)


def levels_iota():
    return lax.broadcasted_iota(jnp.int32, VREG, 0)


def roll_x(v, shift):
    shift %= COLS
    return v if shift == 0 else pltpu.roll(v, shift, 1)


def roll_k(v, shift):
    return pltpu.roll(v, shift % KZ, 0)


def load_row(ref, y):
    return ref[pl.ds(y, KZ, stride=ROWS), :]


def load_tracer(ref, t, y):
    return ref[t, pl.ds(y, KZ, stride=ROWS), :]


def load_wet(land_ref, levels_ref, y):
    depth = jnp.where(land_ref[pl.ds(y, 1), :] == 1, levels_ref[pl.ds(y, 1), :], 0)
    return jnp.where(levels_iota() < jnp.broadcast_to(depth, VREG), 1.0, 0.0)


def halo_row(r):
    return -1 - r if r < HALO else ROWS + r - HALO


def gather_edges(parts):
    slot = ((lanes() - 16) >> 5) & 3
    out = roll_x(parts[-1], 32 * len(parts))
    for t in range(len(parts) - 1):
        out = jnp.where(slot == t, roll_x(parts[t], 32 * (t + 1)), out)
    return out


def pick(v, index):
    return jnp.take_along_axis(v, index, axis=1)


def edge_index(slot, r=0):
    lane = lanes()
    at = (lane - 24) & 31
    field = ((lane - 24) & 96) if slot is None else 32 * slot
    return (field + 4 * r + jnp.where(at < 16, at + 24, at + 8)) & (COLS - 1)


def edge_fields(moving, static, r=0):
    out = [pick(moving, edge_index(None, r))]
    return out + [pick(static, edge_index(f, r)) for f in range(3)]


def pack_eight(rows):
    lane = lanes()
    to_right = ((lane - 28) >> 2) & 7
    to_left = (lane >> 2) & 7
    right = left = rows[0]
    for r in range(1, 8):
        moved = roll_x(rows[r], 4 * r)
        right = jnp.where(to_right == r, moved, right)
        left = jnp.where(to_left == r, moved, left)
    return right, left


def is_even(axis):
    return lax.rem(lax.axis_index(axis), 2) == 0


def meets_fold():
    return lax.axis_index("lat") >= lax.axis_size("lat") - 2


def pack_lat_kernel(tracers, zonal, merid, land, levels, b_ref, a_ref, masks, sems):
    even = is_even("lat")
    pairs = []
    for i, field in enumerate((land, levels)):
        pairs += [
            (field.at[pl.ds(y, 8), :], masks.at[i, side])
            for side, y in enumerate((0, ROWS - 8))
        ]
    sides = ((a_ref, even), (b_ref, jnp.logical_not(even)))
    for ref, at_top in sides:
        flat = ref.reshape(PAYLOAD * KZ, COLS)
        for j in range(HALO):
            y = jnp.where(at_top, ROWS - 1 - j, j)
            pairs.append((tracers.at[:, y, :], flat.at[pl.ds(NT * KZ * j, NT * KZ), :]))
            if j < 3:
                pairs.append((merid.at[:, y, :], ref.at[MERID_AT + j]))
            if j < 2:
                pairs.append((zonal.at[:, y, :], ref.at[ZONAL_AT + j]))
    for copy in start_all(pairs, sems):
        copy.wait()
    for ref, at_top in sides:
        for j in range(HALO):
            row = pl.ds(jnp.where(at_top, 7 - j, j), 1)
            for i in range(2):
                mask = masks[i, jnp.where(at_top, 1, 0), row, :].astype(jnp.float32)
                ref[MASK_AT, HALO * i + j : HALO * i + j + 1, :] = mask

    @pl.when(lax.axis_index("lat") == lax.axis_size("lat") - 1)
    def _():
        flip = COLS - 1 - lanes()
        for p in range(PAYLOAD):
            v = pick(b_ref[p], flip)
            b_ref[p] = v if p < MERID_AT else -v


def start_all(pairs, sems, first=0):
    copies = [
        pltpu.make_async_copy(source, target, sems.at[first + i])
        for i, (source, target) in enumerate(pairs)
    ]
    for copy in copies:
        copy.start()
    return copies


def own_kernel(
    tracers, zonal, merid, land, levels, c0, c1, raw, stat, edge_ref, a_ref, b_ref,
    tracers_here, zonal_here, merid_here, land_here, levels_here, sems, rolled, east
):
    fields = start_all(
        [(land, land_here), (levels, levels_here), (zonal, zonal_here), (merid, merid_here)],
        sems,
    )
    parts = start_all([(tracers, tracers_here)], sems, len(fields))
    level_rows = [v.reshape(KZ * ROWS, COLS) for v in (zonal_here, merid_here)]
    tracer_rows = tracers_here.reshape(NT, KZ * ROWS, COLS)
    even = is_even("lon")

    def pack(i, g, rows):
        right, left = pack_eight(rows)
        a_ref[i, g] = jnp.where(even, right, left)
        b_ref[i, g] = jnp.where(even, left, right)

    for copy in fields:
        copy.wait()

    for g in range(ROWS // 8):
        static = []
        for r in range(8):
            y = 8 * g + r
            row = [load_row(v, y) for v in level_rows] + [load_wet(land_here, levels_here, y)]
            for f in range(3):
                raw[y + HALO, f] = row[f]
            static.append(gather_edges(row))
        pack(1, g, static)
        for r in range(8):
            for f in range(3):
                edge_ref[8 * g + r, 1 + f] = pick(static[r], edge_index(f))
    statics(raw, stat, 1, ROWS - 2, 15, 14)
    for copy in parts:
        copy.wait()

    for g in range(ROWS // 8):
        moving = []
        for r in range(8):
            y = 8 * g + r
            row = [load_tracer(tracer_rows, t, y) for t in range(NT)]
            for t in range(NT):
                c0[y + HALO, t] = row[t]
            moving.append(gather_edges(row))
        pack(0, g, moving)
        for r in range(8):
            edge_ref[8 * g + r, 0] = pick(moving[r], edge_index(None))

    @pl.when(jnp.logical_not(meets_fold()))
    def _():
        advance_rows(c0, stat, rolled, east, NT, 2, ROWS - 2, BLOCK_1, keep_in(c1))


def pack_lon_kernel(
    rb_ref, ra_ref, pa_ref, pb_ref, a_ref, b_ref, d_ref, c_ref, q_ref, static_ref, moving_ref
):
    even_lon = is_even("lon")
    even_lat = is_even("lat")
    bottom = lax.axis_index("lat") == 0
    moving, static = [], []
    for r in range(8):
        j = r % HALO

        def get(p):
            north, south = (ra_ref, rb_ref) if r >= HALO else (rb_ref, ra_ref)
            v = jnp.where(even_lat, north[p], south[p])
            return v if r >= HALO else jnp.where(bottom, 0.0, v)

        cs = [get(NT * j + t) for t in range(NT)]
        mask = get(MASK_AT)
        sea, depth = mask[j : j + 1], mask[HALO + j : HALO + j + 1]
        depth = jnp.broadcast_to(jnp.where(sea == 1.0, depth, 0.0), VREG)
        wet = jnp.where(levels_iota().astype(jnp.float32) < depth, 1.0, 0.0)
        zero = jnp.zeros(VREG, jnp.float32)
        qs = [
            get(ZONAL_AT + j) if j < 2 else zero,
            get(MERID_AT + j) if j < 3 else zero,
            wet,
        ]
        for t in range(NT):
            c_ref[r, t] = cs[t]
        for f in range(3):
            q_ref[r, f] = qs[f]
        moving.append(gather_edges(cs))
        static.append(gather_edges(qs))
        moving_ref[r] = moving[r]
        static_ref[r] = static[r]
    for i, rows in enumerate((moving, static)):
        right, left = pack_eight(rows)
        a_ref[i, ROWS // 8] = d_ref[i, ROWS // 8] = jnp.where(even_lon, right, left)
        b_ref[i, ROWS // 8] = jnp.where(even_lon, left, right)
        for g in range(ROWS // 8):
            a_ref[i, g] = d_ref[i, g] = pa_ref[i, g]
            b_ref[i, g] = pb_ref[i, g]


def derive_along(flow, face, face_before, face_after):
    up = jnp.maximum(flow, 0.0) * (UPSTREAM / 2)
    down = jnp.minimum(flow, 0.0) * (UPSTREAM / 2)
    near = (up - down) + DIFF_H * face
    mean = 0.25 * flow
    far_before, far_after = up * face_before, down * face_after
    return mean + near + far_before, mean - near + far_after, far_before, far_after


def derive(zonal, merid, wet):
    here = wet[1]
    face = here * roll_x(here, -1)
    flow = (zonal + roll_x(zonal, -1)) * face
    along_x = derive_along(flow, face, roll_x(face, 1), roll_x(face, -1))
    faces = [wet[d] * wet[d + 1] for d in range(3)]
    flow = (merid[0] + merid[1]) * faces[1]
    along_y = derive_along(flow, faces[1], faces[0], faces[2])
    face_z = jnp.where(levels_iota() < KZ - 1, here * roll_k(here, -1), 0.0)
    return along_x + along_y + (DIFF_V * face_z, here)


X, Y, FZ, WET = 0, 4, 8, 9


def statics_block(raw, stat, y, block):
    merid = [raw[y, 1]]
    wet = [raw[y + d, 2] for d in range(-1, 2)]
    rows = []
    for d in range(block):
        merid = merid[-1:] + [raw[y + d + 1, 1]]
        wet = wet[-3:] + [raw[y + d + 2, 2]]
        rows.append(derive(raw[y + d, 0], merid, wet))

    def store():
        for d in range(block):
            for f in range(FIELDS):
                stat[y + d, f] = rows[d][f]

    return store


def statics(raw, stat, first, last, block, stride):
    count = (last - first - block) // stride + 1
    assert (count - 1) * stride + block == last - first

    def body(i, _):
        statics_block(raw, stat, first + HALO + i * stride, block)()
        return 0

    lax.fori_loop(0, count, body, 0)


def flux(st, at, before, low, high, after):
    return (st[at] * low + st[at + 1] * high) - (st[at + 2] * before + st[at + 3] * after)


def advance_rows(src, stat, rolled, east, streams, first, last, block, put):
    count = (last - first) // block
    assert count * block == last - first
    every = [(d, s) for d in range(block) for s in range(streams)]

    def shift(y, at):
        for d, s in every:
            here = src[y + d, s]
            for n, v in enumerate([roll_x(here, n) for n in (1, -1, -2)]):
                rolled[at + d, s, n] = v

    def eastward(y, at):
        st = [[stat[y + d, X + f] for f in range(4)] for d in range(block)]
        for d, s in every:
            before, after, far = [rolled[at + d, s, n] for n in range(3)]
            through = flux(st[d], 0, before, src[y + d, s], after, far)
            east[at + d, s, 0] = through
            east[at + d, s, 1] = roll_x(through, 1)

    def total(y, at, below):
        below = list(below)
        c = [[src[y + d, s] for s in range(streams)] for d in range(-2, 2)]
        rows = []
        for d in range(block):
            st = [stat[y + d, f] for f in range(Y, FIELDS)]
            c = c[1:] + [[src[y + d + 2, s] for s in range(streams)]]
            values = []
            for s in range(streams):
                here = c[1][s]
                above = flux(st, 0, c[0][s], here, c[2][s], c[3][s])
                gz = (roll_k(here, -1) - here) * st[FZ - Y]
                along_x = east[at + d, s, 1] - east[at + d, s, 0]
                sum_xy = (here + along_x) + (below[s] - above)
                values.append(st[WET - Y] * (sum_xy + (gz - roll_k(gz, 1))))
                below[s] = above
            rows.append(values)
        for d in range(block):
            put(y - HALO + d, rows[d])
        return tuple(below)

    y = first + HALO
    st = [stat[y - 1, Y + f] for f in range(4)]
    below = tuple(
        flux(st, 0, *[src[y + d, s] for d in range(-2, 2)]) for s in range(streams)
    )
    shift(y, 0)
    if count == 1:
        eastward(y, 0)
        total(y, 0, below)
        return
    if count % 2:
        eastward(y, 0)
        below = total(y, 0, below)
        y += block
        shift(y, 0)

    def body(i, below):
        for half in range(2):
            at = y + (2 * i + half) * block
            here, there = block * half, block * (1 - half)
            eastward(at, here)
            shift(jnp.minimum(at + block, last + HALO - block), there)
            below = total(at, here, below)
        return below

    lax.fori_loop(0, count // 2, body, below)


def keep_in(ref):
    def put(y, values):
        for s, v in enumerate(values):
            ref[y + HALO, s] = v

    return put


def native_in(ref):
    def put(y, values):
        for t, v in enumerate(values):
            ref[t, pl.ds(y, KZ, stride=ROWS), :] = v

    return put


def border_kernel(
    _c0, _c1, _raw, _stat, ch_ref, qh_ref, mh_ref, sh_ref, c0, c1, raw, stat, main_ref, eh_ref,
    rolled, east
):
    for r in range(8):
        y = halo_row(r) + HALO
        for t in range(NT):
            c0[y, t] = ch_ref[r, t]
        for f in range(3):
            raw[y, f] = qh_ref[r, f]
    for store in [statics_block(raw, stat, y + HALO, 4) for y in (-3, ROWS - 2)]:
        store()

    @pl.when(meets_fold())
    def _():
        advance_rows(c0, stat, rolled, east, NT, 2, ROWS - 2, BLOCK_1, keep_in(c1))

    for first in (-2, ROWS - 2):
        advance_rows(c0, stat, rolled, east, NT, first, first + 4, 4, keep_in(c1))
    advance_rows(c1, stat, rolled, east, NT, 4, ROWS - 4, BLOCK_2, native_in(main_ref))
    for first in (0, ROWS - 4):
        advance_rows(c1, stat, rolled, east, NT, first, first + 4, 4, native_in(main_ref))
    for r in range(8):
        for i, v in enumerate(edge_fields(mh_ref[r], sh_ref[r])):
            eh_ref[r, i] = v


BLOCK_1 = 14
BLOCK_2 = 12
EDGE_BLOCK_1 = 36
EDGE_BLOCK_2 = 32


def edge_kernel(
    main_ref, edge_ref, eh_ref, ra_ref, rb_ref, rc_ref, out_ref, e0, e1, raw, stat, native,
    rolled, east
):
    even = is_even("lon")
    last = is_last_pair(lax.axis_index("lon"), lax.axis_size("lon"))
    lane = lanes()
    from_left = ((lane - 28) >> 2) & 7
    at = (lane - 24) & 31
    own = (at < 8) | (at >= 24)
    for g in range(ROWS // 8 + 1):
        evens = [jnp.where(last, rc_ref[i, g], ra_ref[i, g]) for i in range(2)]
        left = [jnp.where(even, rb_ref[i, g], evens[i]) for i in range(2)]
        right = [jnp.where(even, evens[i], rb_ref[i, g]) for i in range(2)]
        both = [
            [jnp.where(from_left == r, left[i], right[i]) for i in range(2)] for r in range(8)
        ]
        for i in range(4):
            other = [
                pick(both[r][min(i, 1)], edge_index(None if i == 0 else i - 1, r))
                for r in range(8)
            ]
            for r in range(8):
                edge, at = (edge_ref, 8 * g + r) if g < ROWS // 8 else (eh_ref, r)
                y = (8 * g + r if g < ROWS // 8 else halo_row(r)) + HALO
                v = jnp.where(own, edge[at, i], other[r])
                if i == 0:
                    e0[y, 0] = v
                else:
                    raw[y, i - 1] = v
    statics(raw, stat, -3, ROWS + 2, 19, 18)

    advance_rows(e0, stat, rolled, east, 1, -2, ROWS + 2, EDGE_BLOCK_1, keep_in(e1))
    high = (lane & 31) >= 16

    def finish(y, values):
        native[pl.ds(y, KZ, stride=ROWS), :] = jnp.where(
            high, values[0], roll_x(values[0], -16)
        )

    advance_rows(e1, stat, rolled, east, 1, 0, ROWS, EDGE_BLOCK_2, finish)
    near = (lane < 4) | (lane >= COLS - 4)
    for i in range(KZ * ROWS // 8):
        edge = native[8 * i : 8 * i + 8, :]
        for t in range(NT):
            out_ref[t, 8 * i : 8 * i + 8, :] = jnp.where(
                near, roll_x(edge, -32 * (t + 1)), main_ref[t, 8 * i : 8 * i + 8, :]
            )


def neighbour_swaps(size, odd, wrap):
    pairs = []
    for i in range(size):
        j = i + 1 if i % 2 == int(odd) else i - 1
        if wrap or 0 <= j < size:
            pairs.append((i, j % size))
    return pairs


def odd_lat_swaps(n_lon, n_lat):
    pairs = []
    for lon in range(n_lon):
        for i, j in neighbour_swaps(n_lat, True, False):
            pairs.append((lon * n_lat + i, lon * n_lat + j))
        pairs.append((lon * n_lat + n_lat - 1, (n_lon - 1 - lon) * n_lat + n_lat - 1))
        pairs.append((lon * n_lat, (lon ^ 1) * n_lat))
    return pairs


def is_last_pair(lon, n_lon):
    return lon % (n_lon // 2) >= n_lon // 2 - 2


def even_lon_swaps(n_lon, n_lat, last):
    pairs = []
    for lon in range(n_lon):
        for lat in range(n_lat):
            mine = is_last_pair(lon, n_lon) == last
            to = (lon ^ 1, lat) if mine else (lon, lat ^ 1)
            pairs.append((lon * n_lat + lat, to[0] * n_lat + to[1]))
    return pairs


def work(streams, values):
    return pltpu.VMEM((EXT, streams, values) + VREG, jnp.float32)


def call(kernel, name, outs, scratch, flops, *args, aliases={}, in_hbm=False):
    f32 = jnp.float32
    kwargs = {}
    if in_hbm:
        args = [pltpu.with_memory_space_constraint(a, pltpu.HBM) for a in args]
        kwargs = dict(in_specs=[pl.BlockSpec(memory_space=pltpu.HBM)] * len(args))
    with jax.named_scope(name):
        return pl.pallas_call(
            kernel,
            out_shape=tuple(jax.ShapeDtypeStruct(tuple(o), f32) for o in outs),
            scratch_shapes=scratch,
            input_output_aliases=aliases,
            compiler_params=pltpu.CompilerParams(vmem_limit_bytes=VMEM_LIMIT),
            cost_estimate=pl.CostEstimate(
                flops=flops,
                bytes_accessed=sum(4 * a.size for a in args),
                transcendentals=0,
            ),
            **kwargs,
        )(*args)


def per_device(tracers, zonal, merid, land, levels):
    axes = ("lon", "lat")
    n_lon, n_lat = lax.axis_size("lon"), lax.axis_size("lat")
    f32 = jnp.float32
    args = (tracers.reshape(NT * KZ, ROWS, COLS), zonal, merid, land, levels)
    groups = ROWS // 8
    native = (NT, KZ * ROWS, COLS)
    mb, ma = call(
        pack_lat_kernel,
        "pack_lat",
        [(PAYLOAD,) + VREG] * 2,
        [
            pltpu.VMEM((2, 2, 8, COLS), jnp.int32),
            pltpu.SemaphoreType.DMA((4 + 2 * (HALO + 3 + 2),)),
        ],
        10**5,
        *args,
        in_hbm=True,
    )
    with jax.named_scope("swap_lat"):
        sb = lax.ppermute(mb, axes, odd_lat_swaps(n_lon, n_lat))
        sa = lax.ppermute(ma, "lat", neighbour_swaps(n_lat, False, False))
    rows = [(EXT, NT) + VREG, (EXT, NT) + VREG, (EXT, 3) + VREG, (EXT, FIELDS) + VREG]
    c0, c1, raw, stat, edge, pa, pb = call(
        own_kernel,
        "interior",
        rows + [(ROWS, 4) + VREG, (2, groups) + VREG, (2, groups) + VREG],
        [
            *[pltpu.VMEM(a.shape, a.dtype) for a in args],
            pltpu.SemaphoreType.DMA((len(args),)),
            work(NT, 3),
            work(NT, 2),
        ],
        10**7,
        *args,
        in_hbm=True,
    )
    la, lb, ld, ch, qh, sh, mh = call(
        pack_lon_kernel,
        "pack_lon",
        [(2, groups + 1) + VREG] * 3
        + [(8, NT) + VREG, (8, 3) + VREG, (8,) + VREG, (8,) + VREG],
        [],
        10**5,
        sb,
        sa,
        pa,
        pb,
    )
    with jax.named_scope("swap_lon"):
        ta = lax.ppermute(la, axes, even_lon_swaps(n_lon, n_lat, False))
        tb = lax.ppermute(lb, "lon", neighbour_swaps(n_lon, True, True))
        tc = lax.ppermute(ld, axes, even_lon_swaps(n_lon, n_lat, True))
    *_, main, eh = call(
        border_kernel,
        "border",
        rows + [native, (8, 4) + VREG],
        [work(NT, 3), work(NT, 2)],
        10**7,
        c0,
        c1,
        raw,
        stat,
        ch,
        qh,
        mh,
        sh,
        aliases={i: i for i in range(4)},
    )
    (out,) = call(
        edge_kernel,
        "edges",
        [native],
        [
            pltpu.VMEM((EXT, 1) + VREG, f32),
            pltpu.VMEM((EXT, 1) + VREG, f32),
            pltpu.VMEM((EXT, 3) + VREG, f32),
            pltpu.VMEM((EXT, FIELDS) + VREG, f32),
            pltpu.VMEM((KZ * ROWS, COLS), f32),
            work(1, 3),
            work(1, 2),
        ],
        10**6,
        main,
        edge,
        eh,
        ta,
        tb,
        tc,
    )
    return out.reshape(tracers.shape)


def solution(mesh):
    return jax.shard_map(
        per_device,
        mesh=mesh,
        in_specs=(
            P(None, None, "lat", "lon"),
            P(None, "lat", "lon"),
            P(None, "lat", "lon"),
            P("lat", "lon"),
            P("lat", "lon"),
        ),
        out_specs=P(None, None, "lat", "lon"),
        check_vma=False,
    )
```

```python
import jax
import jax.numpy as jnp
from jax import lax
from jax.experimental import pallas as pl
from jax.experimental.pallas import tpu as pltpu
from jax.sharding import PartitionSpec as P


KZ = 8
ROWS = 32
COLS = 128
NT = 4
HALO = 4
EXT = ROWS + 2 * HALO
PAYLOAD = 22
MASK_AT = 16
MERID_AT = 17
ZONAL_AT = 20
FIELDS = 10
VMEM_LIMIT = 12 * 2**20

DIFF_H = 0.1
DIFF_V = 0.2
UPSTREAM = 1.0 / 6.0

VREG = (KZ, COLS)


def lanes():
    return lax.broadcasted_iota(jnp.int32, VREG, 1)


def levels_iota():
    return lax.broadcasted_iota(jnp.int32, VREG, 0)


def roll_x(v, shift):
    shift %= COLS
    return v if shift == 0 else pltpu.roll(v, shift, 1)


def roll_k(v, shift):
    return pltpu.roll(v, shift % KZ, 0)


def load_row(ref, y):
    return ref[pl.ds(y, KZ, stride=ROWS), :]


def load_tracer(ref, t, y):
    return ref[t, pl.ds(y, KZ, stride=ROWS), :]


def load_wet(land_ref, levels_ref, y):
    depth = jnp.where(land_ref[pl.ds(y, 1), :] == 1, levels_ref[pl.ds(y, 1), :], 0)
    return jnp.where(levels_iota() < jnp.broadcast_to(depth, VREG), 1.0, 0.0)


def halo_row(r):
    return -1 - r if r < HALO else ROWS + r - HALO


def gather_edges(parts):
    slot = ((lanes() - 16) >> 5) & 3
    out = roll_x(parts[-1], 32 * len(parts))
    for t in range(len(parts) - 1):
        out = jnp.where(slot == t, roll_x(parts[t], 32 * (t + 1)), out)
    return out


def pick(v, index):
    return jnp.take_along_axis(v, index, axis=1)


def edge_index(slot, r=0):
    lane = lanes()
    at = (lane - 24) & 31
    field = ((lane - 24) & 96) if slot is None else 32 * slot
    return (field + 4 * r + jnp.where(at < 16, at + 24, at + 8)) & (COLS - 1)


def edge_fields(moving, static, r=0):
    out = [pick(moving, edge_index(None, r))]
    return out + [pick(static, edge_index(f, r)) for f in range(3)]


def pack_eight(rows):
    lane = lanes()
    to_right = ((lane - 28) >> 2) & 7
    to_left = (lane >> 2) & 7
    right = left = rows[0]
    for r in range(1, 8):
        moved = roll_x(rows[r], 4 * r)
        right = jnp.where(to_right == r, moved, right)
        left = jnp.where(to_left == r, moved, left)
    return right, left


def is_even(axis):
    return lax.rem(lax.axis_index(axis), 2) == 0


def meets_fold():
    return lax.axis_index("lat") >= lax.axis_size("lat") - 2


def pack_lat_kernel(tracers, zonal, merid, land, levels, b_ref, a_ref, masks, sems):
    even = is_even("lat")
    pairs = []
    for i, field in enumerate((land, levels)):
        pairs += [
            (field.at[pl.ds(y, 8), :], masks.at[i, side])
            for side, y in enumerate((0, ROWS - 8))
        ]
    sides = ((a_ref, even), (b_ref, jnp.logical_not(even)))
    for ref, at_top in sides:
        flat = ref.reshape(PAYLOAD * KZ, COLS)
        for j in range(HALO):
            y = jnp.where(at_top, ROWS - 1 - j, j)
            pairs.append((tracers.at[:, y, :], flat.at[pl.ds(NT * KZ * j, NT * KZ), :]))
            if j < 3:
                pairs.append((merid.at[:, y, :], ref.at[MERID_AT + j]))
            if j < 2:
                pairs.append((zonal.at[:, y, :], ref.at[ZONAL_AT + j]))
    for copy in start_all(pairs, sems):
        copy.wait()
    for ref, at_top in sides:
        for j in range(HALO):
            row = pl.ds(jnp.where(at_top, 7 - j, j), 1)
            for i in range(2):
                mask = masks[i, jnp.where(at_top, 1, 0), row, :].astype(jnp.float32)
                ref[MASK_AT, HALO * i + j : HALO * i + j + 1, :] = mask

    @pl.when(lax.axis_index("lat") == lax.axis_size("lat") - 1)
    def _():
        flip = COLS - 1 - lanes()
        for p in range(PAYLOAD):
            v = pick(b_ref[p], flip)
            b_ref[p] = v if p < MERID_AT else -v


def start_all(pairs, sems, first=0):
    copies = [
        pltpu.make_async_copy(source, target, sems.at[first + i])
        for i, (source, target) in enumerate(pairs)
    ]
    for copy in copies:
        copy.start()
    return copies


def own_kernel(
    tracers, zonal, merid, land, levels, c0, c1, raw, stat, main_ref, edge_ref, a_ref, b_ref,
    tracers_here, zonal_here, merid_here, land_here, levels_here, sems, rolled, east
):
    fields = start_all(
        [(land, land_here), (levels, levels_here), (zonal, zonal_here), (merid, merid_here)],
        sems,
    )
    parts = start_all([(tracers, tracers_here)], sems, len(fields))
    level_rows = [v.reshape(KZ * ROWS, COLS) for v in (zonal_here, merid_here)]
    tracer_rows = tracers_here.reshape(NT, KZ * ROWS, COLS)
    even = is_even("lon")

    def pack(i, g, rows):
        right, left = pack_eight(rows)
        a_ref[i, g] = jnp.where(even, right, left)
        b_ref[i, g] = jnp.where(even, left, right)

    for copy in fields:
        copy.wait()

    for g in range(ROWS // 8):
        static = []
        for r in range(8):
            y = 8 * g + r
            row = [load_row(v, y) for v in level_rows] + [load_wet(land_here, levels_here, y)]
            for f in range(3):
                raw[y + HALO, f] = row[f]
            static.append(gather_edges(row))
        pack(1, g, static)
        for r in range(8):
            for f in range(3):
                edge_ref[8 * g + r, 1 + f] = pick(static[r], edge_index(f))
    for copy in parts:
        copy.wait()

    for g in range(ROWS // 8):
        moving = []
        for r in range(8):
            y = 8 * g + r
            row = [load_tracer(tracer_rows, t, y) for t in range(NT)]
            for t in range(NT):
                c0[y + HALO, t] = row[t]
            moving.append(gather_edges(row))
        pack(0, g, moving)
        for r in range(8):
            edge_ref[8 * g + r, 0] = pick(moving[r], edge_index(None))

    @pl.when(jnp.logical_not(meets_fold()))
    def _():
        statics(raw, stat, 1, ROWS - 2, 15, 14)
        advance_rows(c0, stat, rolled, east, NT, 2, ROWS - 2, BLOCK_1, keep_in(c1))
        advance_rows(c1, stat, rolled, east, NT, 4, ROWS - 4, BLOCK_2, native_in(main_ref))


def pack_lon_kernel(
    rb_ref, ra_ref, pa_ref, pb_ref, a_ref, b_ref, d_ref, c_ref, q_ref, static_ref, moving_ref
):
    even_lon = is_even("lon")
    even_lat = is_even("lat")
    bottom = lax.axis_index("lat") == 0
    moving, static = [], []
    for r in range(8):
        j = r % HALO

        def get(p):
            north, south = (ra_ref, rb_ref) if r >= HALO else (rb_ref, ra_ref)
            v = jnp.where(even_lat, north[p], south[p])
            return v if r >= HALO else jnp.where(bottom, 0.0, v)

        cs = [get(NT * j + t) for t in range(NT)]
        mask = get(MASK_AT)
        sea, depth = mask[j : j + 1], mask[HALO + j : HALO + j + 1]
        depth = jnp.broadcast_to(jnp.where(sea == 1.0, depth, 0.0), VREG)
        wet = jnp.where(levels_iota().astype(jnp.float32) < depth, 1.0, 0.0)
        zero = jnp.zeros(VREG, jnp.float32)
        qs = [
            get(ZONAL_AT + j) if j < 2 else zero,
            get(MERID_AT + j) if j < 3 else zero,
            wet,
        ]
        for t in range(NT):
            c_ref[r, t] = cs[t]
        for f in range(3):
            q_ref[r, f] = qs[f]
        moving.append(gather_edges(cs))
        static.append(gather_edges(qs))
        moving_ref[r] = moving[r]
        static_ref[r] = static[r]
    for i, rows in enumerate((moving, static)):
        right, left = pack_eight(rows)
        a_ref[i, ROWS // 8] = d_ref[i, ROWS // 8] = jnp.where(even_lon, right, left)
        b_ref[i, ROWS // 8] = jnp.where(even_lon, left, right)
        for g in range(ROWS // 8):
            a_ref[i, g] = d_ref[i, g] = pa_ref[i, g]
            b_ref[i, g] = pb_ref[i, g]


def derive_along(flow, face, face_before, face_after):
    up = jnp.maximum(flow, 0.0) * (UPSTREAM / 2)
    down = jnp.minimum(flow, 0.0) * (UPSTREAM / 2)
    near = (up - down) + DIFF_H * face
    mean = 0.25 * flow
    far_before, far_after = up * face_before, down * face_after
    return mean + near + far_before, mean - near + far_after, far_before, far_after


def derive(zonal, merid, wet):
    here = wet[1]
    face = here * roll_x(here, -1)
    flow = (zonal + roll_x(zonal, -1)) * face
    along_x = derive_along(flow, face, roll_x(face, 1), roll_x(face, -1))
    faces = [wet[d] * wet[d + 1] for d in range(3)]
    flow = (merid[0] + merid[1]) * faces[1]
    along_y = derive_along(flow, faces[1], faces[0], faces[2])
    face_z = jnp.where(levels_iota() < KZ - 1, here * roll_k(here, -1), 0.0)
    return along_x + along_y + (DIFF_V * face_z, here)


X, Y, FZ, WET = 0, 4, 8, 9


def statics_block(raw, stat, y, block):
    merid = [raw[y, 1]]
    wet = [raw[y + d, 2] for d in range(-1, 2)]
    rows = []
    for d in range(block):
        merid = merid[-1:] + [raw[y + d + 1, 1]]
        wet = wet[-3:] + [raw[y + d + 2, 2]]
        rows.append(derive(raw[y + d, 0], merid, wet))

    def store():
        for d in range(block):
            for f in range(FIELDS):
                stat[y + d, f] = rows[d][f]

    return store


def statics(raw, stat, first, last, block, stride):
    count = (last - first - block) // stride + 1
    assert (count - 1) * stride + block == last - first

    def body(i, _):
        statics_block(raw, stat, first + HALO + i * stride, block)()
        return 0

    lax.fori_loop(0, count, body, 0)


def flux(st, at, before, low, high, after):
    return (st[at] * low + st[at + 1] * high) - (st[at + 2] * before + st[at + 3] * after)


def advance_rows(src, stat, rolled, east, streams, first, last, block, put):
    count = (last - first) // block
    assert count * block == last - first
    every = [(d, s) for d in range(block) for s in range(streams)]

    def shift(y, at):
        for d, s in every:
            here = src[y + d, s]
            for n, v in enumerate([roll_x(here, n) for n in (1, -1, -2)]):
                rolled[at + d, s, n] = v

    def eastward(y, at):
        st = [[stat[y + d, X + f] for f in range(4)] for d in range(block)]
        for d, s in every:
            before, after, far = [rolled[at + d, s, n] for n in range(3)]
            through = flux(st[d], 0, before, src[y + d, s], after, far)
            east[at + d, s, 0] = through
            east[at + d, s, 1] = roll_x(through, 1)

    def total(y, at, below):
        below = list(below)
        c = [[src[y + d, s] for s in range(streams)] for d in range(-2, 2)]
        rows = []
        for d in range(block):
            st = [stat[y + d, f] for f in range(Y, FIELDS)]
            c = c[1:] + [[src[y + d + 2, s] for s in range(streams)]]
            values = []
            for s in range(streams):
                here = c[1][s]
                above = flux(st, 0, c[0][s], here, c[2][s], c[3][s])
                gz = (roll_k(here, -1) - here) * st[FZ - Y]
                along_x = east[at + d, s, 1] - east[at + d, s, 0]
                sum_xy = (here + along_x) + (below[s] - above)
                values.append(st[WET - Y] * (sum_xy + (gz - roll_k(gz, 1))))
                below[s] = above
            rows.append(values)
        for d in range(block):
            put(y - HALO + d, rows[d])
        return tuple(below)

    y = first + HALO
    st = [stat[y - 1, Y + f] for f in range(4)]
    below = tuple(
        flux(st, 0, *[src[y + d, s] for d in range(-2, 2)]) for s in range(streams)
    )
    shift(y, 0)
    if count == 1:
        eastward(y, 0)
        total(y, 0, below)
        return
    if count % 2:
        eastward(y, 0)
        below = total(y, 0, below)
        y += block
        shift(y, 0)

    def body(i, below):
        for half in range(2):
            at = y + (2 * i + half) * block
            here, there = block * half, block * (1 - half)
            eastward(at, here)
            shift(jnp.minimum(at + block, last + HALO - block), there)
            below = total(at, here, below)
        return below

    lax.fori_loop(0, count // 2, body, below)


def keep_in(ref):
    def put(y, values):
        for s, v in enumerate(values):
            ref[y + HALO, s] = v

    return put


def native_in(ref):
    def put(y, values):
        for t, v in enumerate(values):
            ref[t, pl.ds(y, KZ, stride=ROWS), :] = v

    return put


def border_kernel(
    _c0, _c1, _raw, _stat, _main, ch_ref, qh_ref, mh_ref, sh_ref, c0, c1, raw, stat, main_ref, eh_ref,
    rolled, east
):
    for r in range(8):
        y = halo_row(r) + HALO
        for t in range(NT):
            c0[y, t] = ch_ref[r, t]
        for f in range(3):
            raw[y, f] = qh_ref[r, f]
    for store in [statics_block(raw, stat, y + HALO, 4) for y in (-3, ROWS - 2)]:
        store()

    @pl.when(meets_fold())
    def _():
        statics(raw, stat, 1, ROWS - 2, 15, 14)
        advance_rows(c0, stat, rolled, east, NT, 2, ROWS - 2, BLOCK_1, keep_in(c1))
        advance_rows(c1, stat, rolled, east, NT, 4, ROWS - 4, BLOCK_2, native_in(main_ref))

    for first in (-2, ROWS - 2):
        advance_rows(c0, stat, rolled, east, NT, first, first + 4, 4, keep_in(c1))
    for first in (0, ROWS - 4):
        advance_rows(c1, stat, rolled, east, NT, first, first + 4, 4, native_in(main_ref))
    for r in range(8):
        for i, v in enumerate(edge_fields(mh_ref[r], sh_ref[r])):
            eh_ref[r, i] = v


BLOCK_1 = 14
BLOCK_2 = 12
EDGE_BLOCK_1 = 36
EDGE_BLOCK_2 = 32


def edge_kernel(
    main_ref, edge_ref, eh_ref, ra_ref, rb_ref, rc_ref, out_ref, e0, e1, raw, stat, native,
    rolled, east
):
    even = is_even("lon")
    last = is_last_pair(lax.axis_index("lon"), lax.axis_size("lon"))
    lane = lanes()
    from_left = ((lane - 28) >> 2) & 7
    at = (lane - 24) & 31
    own = (at < 8) | (at >= 24)
    for g in range(ROWS // 8 + 1):
        evens = [jnp.where(last, rc_ref[i, g], ra_ref[i, g]) for i in range(2)]
        left = [jnp.where(even, rb_ref[i, g], evens[i]) for i in range(2)]
        right = [jnp.where(even, evens[i], rb_ref[i, g]) for i in range(2)]
        both = [
            [jnp.where(from_left == r, left[i], right[i]) for i in range(2)] for r in range(8)
        ]
        for i in range(4):
            other = [
                pick(both[r][min(i, 1)], edge_index(None if i == 0 else i - 1, r))
                for r in range(8)
            ]
            for r in range(8):
                edge, at = (edge_ref, 8 * g + r) if g < ROWS // 8 else (eh_ref, r)
                y = (8 * g + r if g < ROWS // 8 else halo_row(r)) + HALO
                v = jnp.where(own, edge[at, i], other[r])
                if i == 0:
                    e0[y, 0] = v
                else:
                    raw[y, i - 1] = v
    statics(raw, stat, -3, ROWS + 2, 19, 18)

    advance_rows(e0, stat, rolled, east, 1, -2, ROWS + 2, EDGE_BLOCK_1, keep_in(e1))
    high = (lane & 31) >= 16

    def finish(y, values):
        native[pl.ds(y, KZ, stride=ROWS), :] = jnp.where(
            high, values[0], roll_x(values[0], -16)
        )

    advance_rows(e1, stat, rolled, east, 1, 0, ROWS, EDGE_BLOCK_2, finish)
    near = (lane < 4) | (lane >= COLS - 4)
    for i in range(KZ * ROWS // 8):
        edge = native[8 * i : 8 * i + 8, :]
        for t in range(NT):
            out_ref[t, 8 * i : 8 * i + 8, :] = jnp.where(
                near, roll_x(edge, -32 * (t + 1)), main_ref[t, 8 * i : 8 * i + 8, :]
            )


def neighbour_swaps(size, odd, wrap):
    pairs = []
    for i in range(size):
        j = i + 1 if i % 2 == int(odd) else i - 1
        if wrap or 0 <= j < size:
            pairs.append((i, j % size))
    return pairs


def odd_lat_swaps(n_lon, n_lat):
    pairs = []
    for lon in range(n_lon):
        for i, j in neighbour_swaps(n_lat, True, False):
            pairs.append((lon * n_lat + i, lon * n_lat + j))
        pairs.append((lon * n_lat + n_lat - 1, (n_lon - 1 - lon) * n_lat + n_lat - 1))
        pairs.append((lon * n_lat, (lon ^ 1) * n_lat))
    return pairs


def is_last_pair(lon, n_lon):
    return lon % (n_lon // 2) >= n_lon // 2 - 2


def even_lon_swaps(n_lon, n_lat, last):
    pairs = []
    for lon in range(n_lon):
        for lat in range(n_lat):
            mine = is_last_pair(lon, n_lon) == last
            to = (lon ^ 1, lat) if mine else (lon, lat ^ 1)
            pairs.append((lon * n_lat + lat, to[0] * n_lat + to[1]))
    return pairs


def work(streams, values):
    return pltpu.VMEM((EXT, streams, values) + VREG, jnp.float32)


def call(kernel, name, outs, scratch, flops, *args, aliases={}, in_hbm=False):
    f32 = jnp.float32
    kwargs = {}
    if in_hbm:
        args = [pltpu.with_memory_space_constraint(a, pltpu.HBM) for a in args]
        kwargs = dict(in_specs=[pl.BlockSpec(memory_space=pltpu.HBM)] * len(args))
    with jax.named_scope(name):
        return pl.pallas_call(
            kernel,
            out_shape=tuple(jax.ShapeDtypeStruct(tuple(o), f32) for o in outs),
            scratch_shapes=scratch,
            input_output_aliases=aliases,
            compiler_params=pltpu.CompilerParams(vmem_limit_bytes=VMEM_LIMIT),
            cost_estimate=pl.CostEstimate(
                flops=flops,
                bytes_accessed=sum(4 * a.size for a in args),
                transcendentals=0,
            ),
            **kwargs,
        )(*args)


def per_device(tracers, zonal, merid, land, levels):
    axes = ("lon", "lat")
    n_lon, n_lat = lax.axis_size("lon"), lax.axis_size("lat")
    f32 = jnp.float32
    args = (tracers.reshape(NT * KZ, ROWS, COLS), zonal, merid, land, levels)
    groups = ROWS // 8
    native = (NT, KZ * ROWS, COLS)
    mb, ma = call(
        pack_lat_kernel,
        "pack_lat",
        [(PAYLOAD,) + VREG] * 2,
        [
            pltpu.VMEM((2, 2, 8, COLS), jnp.int32),
            pltpu.SemaphoreType.DMA((4 + 2 * (HALO + 3 + 2),)),
        ],
        10**5,
        *args,
        in_hbm=True,
    )
    with jax.named_scope("swap_lat"):
        sb = lax.ppermute(mb, axes, odd_lat_swaps(n_lon, n_lat))
        sa = lax.ppermute(ma, "lat", neighbour_swaps(n_lat, False, False))
    rows = [(EXT, NT) + VREG, (EXT, NT) + VREG, (EXT, 3) + VREG, (EXT, FIELDS) + VREG]
    c0, c1, raw, stat, main, edge, pa, pb = call(
        own_kernel,
        "interior",
        rows + [native, (ROWS, 4) + VREG, (2, groups) + VREG, (2, groups) + VREG],
        [
            *[pltpu.VMEM(a.shape, a.dtype) for a in args],
            pltpu.SemaphoreType.DMA((len(args),)),
            work(NT, 3),
            work(NT, 2),
        ],
        10**7,
        *args,
        in_hbm=True,
    )
    la, lb, ld, ch, qh, sh, mh = call(
        pack_lon_kernel,
        "pack_lon",
        [(2, groups + 1) + VREG] * 3
        + [(8, NT) + VREG, (8, 3) + VREG, (8,) + VREG, (8,) + VREG],
        [],
        10**5,
        sb,
        sa,
        pa,
        pb,
    )
    with jax.named_scope("swap_lon"):
        ta = lax.ppermute(la, axes, even_lon_swaps(n_lon, n_lat, False))
        tb = lax.ppermute(lb, "lon", neighbour_swaps(n_lon, True, True))
        tc = lax.ppermute(ld, axes, even_lon_swaps(n_lon, n_lat, True))
    *_, main, eh = call(
        border_kernel,
        "border",
        rows + [native, (8, 4) + VREG],
        [work(NT, 3), work(NT, 2)],
        10**7,
        c0,
        c1,
        raw,
        stat,
        main,
        ch,
        qh,
        mh,
        sh,
        aliases={i: i for i in range(5)},
    )
    (out,) = call(
        edge_kernel,
        "edges",
        [native],
        [
            pltpu.VMEM((EXT, 1) + VREG, f32),
            pltpu.VMEM((EXT, 1) + VREG, f32),
            pltpu.VMEM((EXT, 3) + VREG, f32),
            pltpu.VMEM((EXT, FIELDS) + VREG, f32),
            pltpu.VMEM((KZ * ROWS, COLS), f32),
            work(1, 3),
            work(1, 2),
        ],
        10**6,
        main,
        edge,
        eh,
        ta,
        tb,
        tc,
    )
    return out.reshape(tracers.shape)


def solution(mesh):
    return jax.shard_map(
        per_device,
        mesh=mesh,
        in_specs=(
            P(None, None, "lat", "lon"),
            P(None, "lat", "lon"),
            P(None, "lat", "lon"),
            P("lat", "lon"),
            P("lat", "lon"),
        ),
        out_specs=P(None, None, "lat", "lon"),
        check_vma=False,
    )
```
